256 devices in a mesh: grp: 4 (over y), vocab: 32 (over z, x_hi, core), sub: 2 (over x_lo).
Axes of the slice: x: 4 (x_hi: 2, x_lo: 2; x = x_hi * 2 + x_lo), y: 4, z: 8, core: 2. Of those that a mesh axis runs over, the one named last changes fastest.
Arguments:
- teacher_hidden: bfloat16 [512, 16384], P(('vocab', 'sub'), 'grp'), may hold values from -6 to 6
- teacher_head: bfloat16 [16384, 65536], P('grp', ('vocab', 'sub'))
- student_hidden: bfloat16 [512, 8192], P('grp', ('vocab', 'sub')), may hold values from -6 to 6
- student_head: bfloat16 [8192, 65536], P('grp', ('vocab', 'sub'))
- teacher_rest: float32 [512], P('grp'), as said below
- student_rest: float32 [512], P('grp'), as said below
- sampled: int32 [512], replicated, may hold values from 0 to 65535
- assign: int32 [512], replicated, may hold values from 0 to 511, each once
Outputs:
- hidden_grad: bfloat16 [512, 8192], P('grp', ('vocab', 'sub'))
- divergence: float32 [512], P('grp')
- sampled_logprob: float32 [512], P('grp')
The draws below stay inside these ranges and needn't reach their ends.
Inputs may be any that keep to these rules, and one draw needn't show every extreme that they name: `teacher_rest`: each value exceeds the natural logarithm of 65536 by 2.2 to 6.5. `student_rest`: each value exceeds the natural logarithm of 65536 by 2.2 to 6.5.
All inputs are finite; a program needn't handle non-finite values.
Results may differ from the reference program's by a relative error of at most 0.0049.
Values may be sent and summed in bfloat16 or wider, within the bound.
No kernel may reach another device: no remote copies, remote signals or barrier semaphores. Data moves between devices by JAX's collectives and lax.ppermute only.
A program may use at most 128 MiB of HBM per device.

```python
import math
import jax
import jax.numpy as jnp

DT = 16384
DS = 8192
TOKENS = 512
VW = 65536


def scale_columns(normal_part, fan_in, growth):
    column_pos = jnp.arange(normal_part.shape[1], dtype=jnp.float32) / normal_part.shape[1]
    column_rate = 2.5 * jnp.exp(growth * column_pos)
    return normal_part * column_rate[None, :] / math.sqrt(fan_in)


def draw_teacher_head(key, part):
    key = jax.random.fold_in(key, 11)
    normal_part = jnp.clip(jax.random.normal(key, (DT, VW), jnp.float32), -6.0, 6.0)
    growth = 0.14
    return scale_columns(normal_part, DT, growth).astype(jnp.bfloat16)


def draw_student_head(key, part):
    key = jax.random.fold_in(key, 17)
    normal_part = jnp.clip(jax.random.normal(key, (DS, VW), jnp.float32), -6.0, 6.0)
    growth = 0.14
    return scale_columns(normal_part, DS, growth).astype(jnp.bfloat16)


def draw_teacher_rest(key, part):
    key = jax.random.fold_in(key, 23)
    offset_value = jax.random.uniform(key, (TOKENS,), jnp.float32, 2.2, 5.2)
    return (math.log(VW) + offset_value).astype(jnp.float32)


def draw_student_rest(key, part):
    key = jax.random.fold_in(key, 29)
    offset_value = jax.random.uniform(key, (TOKENS,), jnp.float32, 2.2, 5.2)
    return (math.log(VW) + offset_value).astype(jnp.float32)


def plant(entries, stream_key, low, largest):
    longest = entries.shape.index(max(entries.shape))
    spots = []
    for shift in (0, 1):
        where = [jax.random.randint(jax.random.fold_in(stream_key, axis), (), 0, length) for axis, length in enumerate(entries.shape)]
        where[longest] = (where[longest] + shift) % entries.shape[longest]
        spots.append(tuple(where))
    return entries.at[spots[0]].set(low).at[spots[1]].set(largest)


def shard_levels(rng, dims, pieces, least, high):
    loudness = 1.0
    for dim, blocks in pieces:
        heights = jax.random.uniform(jax.random.fold_in(jax.random.fold_in(rng, 6), dim), (blocks,), jnp.float32, least / len(pieces), high / len(pieces))
        loudness = loudness * jnp.repeat(jnp.exp(heights), dims[dim] // blocks).reshape((-1,) + (1,) * (len(dims) - 1 - dim))
    return loudness


def noise(key, shape, deviation, limit, split=(), kind=jnp.bfloat16):
    result = jax.random.normal(key, shape, jnp.float32) * deviation
    if len(split) > 0:
        result = shard_levels(key, shape, split, -0.22, 0.18) * result
    return jnp.clip(result, min=-limit, max=limit).astype(kind)


def setup_inputs(seed: int = 0) -> dict:
    keys = jax.random.split(jax.random.key(seed), 9)
    teacher_hidden = noise(keys[0], (TOKENS, DT), 1.0, 6.0, ((0, 64), (1, 4)))
    teacher_head = draw_teacher_head(jax.random.fold_in(keys[8], 71), 0)
    student_hidden = noise(keys[2], (TOKENS, DS), 1.0, 6.0, ((0, 4), (1, 64)))
    student_head = draw_student_head(jax.random.fold_in(keys[8], 71), 0)
    teacher_rest = draw_teacher_rest(jax.random.fold_in(keys[8], 71), 0)
    student_rest = draw_student_rest(jax.random.fold_in(keys[8], 71), 0)
    sampled = plant(jax.random.randint(keys[6], (TOKENS,), 0, VW), jax.random.fold_in(keys[6], 1), 0, VW - 1).astype(jnp.int32)
    assign = jax.random.permutation(keys[7], TOKENS).astype(jnp.int32)
    return dict(teacher_hidden=teacher_hidden, teacher_head=teacher_head, student_hidden=student_hidden, student_head=student_head, teacher_rest=teacher_rest, student_rest=student_rest, sampled=sampled, assign=assign)


loss_scale = 256.0


def reference(teacher_hidden, teacher_head, student_hidden, student_head, teacher_rest, student_rest, sampled, assign):
    chosen_rows = jnp.take(teacher_hidden, assign, axis=0)
    teacher_logit = jnp.dot(chosen_rows, teacher_head, preferred_element_type=jnp.float32)
    student_logit = jnp.dot(student_hidden, student_head, preferred_element_type=jnp.float32)
    teacher_exp = jnp.exp(teacher_logit)
    student_exp = jnp.exp(student_logit)
    teacher_norm = jnp.log(jnp.sum(teacher_exp, axis=1) + jnp.exp(teacher_rest))
    student_norm = jnp.log(jnp.sum(student_exp, axis=1) + jnp.exp(student_rest))
    teacher_prob = teacher_exp * jnp.exp(-teacher_norm)[:, None]
    student_prob = student_exp * jnp.exp(-student_norm)[:, None]
    token_ids = jnp.take(sampled, assign, axis=0)
    picked = jnp.take_along_axis(student_logit, token_ids[:, None], axis=1)[:, 0]
    sampled_logprob = picked - student_norm
    divergence = jnp.sum(teacher_prob * (teacher_logit - teacher_norm[:, None] - student_logit + student_norm[:, None]), axis=1)
    delta_bf = (loss_scale * (student_prob - teacher_prob)).astype(jnp.bfloat16)
    hidden_grad = jnp.dot(delta_bf, student_head.T, preferred_element_type=jnp.float32).astype(jnp.bfloat16)
    return (hidden_grad, divergence, sampled_logprob)
```

```python
import jax
import jax.numpy as jnp
import numpy as np
from jax import lax
from jax.sharding import Mesh, PartitionSpec as P

loss_scale = 256.0
f32, bf16, i16 = jnp.float32, jnp.bfloat16, jnp.int16

AXES = ("y", "zh", "zl", "xh", "c", "xl")
SIZES = (4, 4, 2, 2, 2, 2)
X = ("xh", "xl")
Z = ("zh", "zl")
VOCAB = ("zh", "zl", "xh", "c", "xl")
NY, NX, NZ = 4, 4, 8


def shift(a, axes, n, k):
    return lax.ppermute(a, axes, [(i, (i + k) % n) for i in range(n)])


def other_core(a):
    return lax.ppermute(a, "c", [(0, 1), (1, 0)])


def turn(a, start, n):
    return lax.dynamic_slice_in_dim(jnp.concatenate([a, a], 0), start, n, 0)


def swap_pairs(k, back):
    pairs = []
    for s in range(4):
        for t in range(4):
            to = ((t + k) % 4, s) if back else (t, (s + k) % 4)
            pairs.append((s * 4 + t, to[0] * 4 + to[1]))
    return pairs


def gather_teacher(rows):
    z, x, c = lax.axis_index(Z), lax.axis_index(X), lax.axis_index("c")
    across = jnp.concatenate([rows] + [shift(rows, X, NX, k) for k in range(1, NX)], 0)
    right = left = across
    pieces, offsets = [across], [0]
    for k in range(1, 5):
        right = shift(right, Z, NZ, 1)
        pieces.append(right)
        offsets.append(-k)
        if k < 4:
            left = shift(left, Z, NZ, -1)
            pieces.append(left)
            offsets.append(k)
    n = rows.shape[0]
    other = [other_core(p) for p in pieces]
    xs = (x - jnp.arange(NX)) % NX
    zs = (z + jnp.array(offsets)) % NZ

    def places(core):
        block = zs[:, None] * 8 + (xs // 2)[None, :] * 4 + core * 2 + (xs % 2)[None, :]
        return (block[:, :, None] * n + jnp.arange(n)).reshape(-1)

    return jnp.concatenate(pieces + other, 0), jnp.concatenate([places(c), places(1 - c)])


def gather_student(block):
    y, zh, zl = lax.axis_index("y"), lax.axis_index("zh"), lax.axis_index("zl")
    x, c = lax.axis_index(X), lax.axis_index("c")
    got = jnp.stack([lax.ppermute(block, ("y", "zh"), swap_pairs(k, False)) for k in range(4)])
    got = turn(got[::-1], 3 - (zh - y) % 4, 4)
    tokens, feats = got.shape[1] * 4, got.shape[2]
    got = got.reshape(tokens, feats)
    mate = lax.ppermute(got, "zl", [(0, 1), (1, 0)])
    got = jnp.where(zl == 0, jnp.stack([got, mate]), jnp.stack([mate, got]))
    got = jnp.stack([shift(got, X, NX, k) for k in (3, 2, 1)] + [got])
    got = turn(got, 3 - x, NX)
    mate = other_core(got)
    got = jnp.where(c == 0, jnp.stack([got, mate]), jnp.stack([mate, got]))
    got = got.reshape(2, 2, 2, 2, tokens, feats)
    return got.transpose(4, 3, 1, 0, 2, 5).reshape(tokens, 16 * feats)


def sum_over_y(part):
    total, cols = part.shape
    rows = total // 4
    top = jnp.max(jnp.abs(part), axis=1)
    power = jnp.clip(jnp.ceil(jnp.log2(jnp.maximum(top, 1e-30)) + 0.001), -90.0, 126.0)
    code = jnp.round(part * (jnp.exp2(-power) * 32766.0)[:, None])
    code = jnp.clip(code, -32767.0, 32767.0).astype(i16).reshape(4, rows, cols)
    tail = jnp.pad(power.astype(i16).reshape(4, 1, rows), ((0, 0), (0, 15), (0, cols - rows)))
    code = jnp.concatenate([code, tail], 1)
    out = part[:rows]
    for k in (2, 1, 3):
        got = shift(code[k], "y", NY, k)
        scale = jnp.exp2(got[rows, :rows].astype(f32)) * (1.0 / 32766.0)
        out = out + got[:rows].astype(f32) * scale[:, None]
    return out


def per_device(
    teacher_hidden,
    teacher_head,
    student_hidden,
    student_head,
    teacher_rest,
    student_rest,
    sampled,
    assign,
):
    y, zh, c = lax.axis_index("y"), lax.axis_index("zh"), lax.axis_index("c")
    tok_rows = student_hidden.shape[0]
    vocab_cols = student_head.shape[1]
    ahead = lax.dynamic_slice_in_dim(
        jnp.concatenate([assign, assign]), y * tok_rows, 4 * tok_rows, 0
    )

    rows_all, places = gather_teacher(teacher_hidden)
    student_all = gather_student(student_hidden)

    pick = (ahead[:, None] == places[None, :]).astype(bf16)
    chosen = jnp.dot(pick, rows_all, preferred_element_type=f32).astype(bf16)
    teacher_logit = sum_over_y(jnp.dot(chosen, teacher_head, preferred_element_type=f32))
    student_logit = sum_over_y(jnp.dot(student_all, student_head, preferred_element_type=f32))

    token_ids = jnp.take(sampled, ahead[:tok_rows], axis=0)
    col_index = lax.axis_index(VOCAB) * vocab_cols + lax.broadcasted_iota(
        jnp.int32, (1, vocab_cols), 1
    )
    teacher_exp = jnp.exp(teacher_logit - teacher_rest[:, None])
    student_exp = jnp.exp(student_logit - student_rest[:, None])
    sums = jnp.stack(
        [
            jnp.sum(teacher_exp, axis=1),
            jnp.sum(student_exp, axis=1),
            jnp.sum(teacher_exp * (teacher_logit - student_logit), axis=1),
            jnp.sum(jnp.where(col_index == token_ids[:, None], student_logit, 0.0), axis=1),
        ]
    )
    sums = lax.all_to_all(jnp.broadcast_to(sums[None], (64,) + sums.shape), VOCAB, 0, 0)
    teacher_total, student_total, gap, picked = jnp.sum(sums, axis=0)
    teacher_norm = teacher_rest + jnp.log(1.0 + teacher_total)
    student_norm = student_rest + jnp.log(1.0 + student_total)
    teacher_scale = 1.0 / (1.0 + teacher_total)
    student_scale = 1.0 / (1.0 + student_total)
    divergence = (gap - (teacher_norm - student_norm) * teacher_total) * teacher_scale
    sampled_logprob = picked - student_norm

    delta = (
        loss_scale * (student_exp * student_scale[:, None] - teacher_exp * teacher_scale[:, None])
    ).astype(bf16)
    half = tok_rows // 2
    behind = shift(delta, "y", NY, 1)
    front = shift(delta, "y", NY, -1)
    far = [shift(behind[:half], "y", NY, 1), shift(front[half:], "y", NY, -1)]
    delta_all = jnp.concatenate([delta, front] + far + [behind], 0)

    grad = lax.dot_general(
        delta_all, student_head, (((1,), (1,)), ((), ())), preferred_element_type=f32
    )
    feats = student_hidden.shape[1]
    grad = grad.reshape(4 * tok_rows, 4, 2, 2 * feats)
    mine = lax.dynamic_index_in_dim(grad, c, 2, keepdims=False)
    theirs = lax.dynamic_index_in_dim(grad, 1 - c, 2, keepdims=False)
    mine = (mine + other_core(theirs)).astype(bf16)
    mine = mine.reshape(4 * tok_rows, 8, feats).transpose(1, 0, 2)
    mine = lax.all_to_all(mine, ("zl", "xh", "xl"), 0, 0)
    mine = jnp.sum(mine.astype(f32), axis=0).reshape(4, tok_rows, feats)
    mine = turn(mine, (zh - y) % 4, 4)
    hidden_grad = sum(lax.ppermute(mine[k], ("y", "zh"), swap_pairs(k, True)) for k in range(4))
    return (hidden_grad.astype(bf16), divergence, sampled_logprob)


def solution(mesh):
    fine = Mesh(np.asarray(mesh.devices).reshape(SIZES), AXES)
    return jax.shard_map(
        per_device,
        mesh=fine,
        in_specs=(
            P(VOCAB, "y"),
            P("y", VOCAB),
            P("y", VOCAB),
            P("y", VOCAB),
            P("y"),
            P("y"),
            P(),
            P(),
        ),
        out_specs=(P("y", VOCAB), P("y"), P("y")),
        check_vma=False,
    )
```

```python
import jax
import jax.numpy as jnp
import numpy as np
from jax import lax
from jax.experimental import pallas as pl
from jax.experimental.pallas import tpu as pltpu
from jax.sharding import Mesh, PartitionSpec as P

loss_scale = 256.0
f32, bf16, i16 = jnp.float32, jnp.bfloat16, jnp.int16

AXES = ("y", "zh", "zl", "xh", "c", "xl")
SIZES = (4, 4, 2, 2, 2, 2)
X = ("xh", "xl")
Z = ("zh", "zl")
VOCAB = ("zh", "zl", "xh", "c", "xl")
NY, NX, NZ = 4, 4, 8
TAIL = 16
TOP = 32766.0
VMEM = 40 * 1024 * 1024


def shift(a, axes, n, k):
    return lax.ppermute(a, axes, [(i, (i + k) % n) for i in range(n)])


def other_core(a):
    return lax.ppermute(a, "c", [(0, 1), (1, 0)])


def turn(a, start, n):
    return lax.dynamic_slice_in_dim(jnp.concatenate([a, a], 0), start, n, 0)


def swap_pairs(k):
    return [(s * 4 + t, t * 4 + (s + k) % 4) for s in range(4) for t in range(4)]


def write_coded(part_ref, code_ref, own_ref):
    rows, cols = own_ref.shape
    own_ref[...] = part_ref[:rows, :]
    diagonal = lax.broadcasted_iota(jnp.int32, (rows, rows), 0) == lax.broadcasted_iota(
        jnp.int32, (rows, rows), 1
    )
    for b in range(1, 4):
        part = part_ref[b * rows : (b + 1) * rows, :]
        top = jnp.max(jnp.abs(part), axis=1, keepdims=True)
        power = jnp.ceil(jnp.log(jnp.maximum(top, 1e-30)) * 1.4426950408889634 + 0.001)
        power = jnp.clip(power, -90.0, 126.0)
        code = jnp.floor(part * (jnp.exp(power * -0.6931471805599453) * TOP) + 0.5)
        code = jnp.clip(code, -32767.0, 32767.0)
        code_ref[b - 1, :rows, :] = code.astype(jnp.int32).astype(i16)
        across = jnp.sum(jnp.where(diagonal, power, 0.0), axis=0, keepdims=True)
        across = jnp.broadcast_to(across, (TAIL, rows))
        code_ref[b - 1, rows:, :rows] = across.astype(jnp.int32).astype(i16)
        if cols > rows:
            code_ref[b - 1, rows:, rows:] = jnp.zeros((TAIL, cols - rows), i16)


def in_hbm(n):
    return [pl.BlockSpec(memory_space=pltpu.HBM)] * n


def in_vmem(n):
    return [pl.BlockSpec(memory_space=pltpu.VMEM)] * n


def stay(a):
    return pltpu.with_memory_space_constraint(a, pltpu.HBM)


def keep(a):
    return pltpu.with_memory_space_constraint(a, pltpu.VMEM)


def fetch(pairs, sems):
    copies = [pltpu.make_async_copy(a, b, sems.at[i]) for i, (a, b) in enumerate(pairs)]
    for copy in copies:
        copy.start()
    return copies


def write_product(acc, source, head):
    tile = acc.shape[0] // 2

    @pl.loop(0, 2)
    def _(i):
        rows = pl.ds(pl.multiple_of(i * tile, tile), tile)
        acc[rows, :] = jnp.dot(source[rows, :], head[...], preferred_element_type=f32)


def teacher_kernel(
    ahead_ref, places_ref, mine_ref, other_ref, head_ref, code_ref, own_ref,
    mine, other, head, chosen, acc, mine_sems, other_sems, head_sems,
):
    half, width = mine_ref.shape
    parts = head_sems.shape[0]
    tile = width // parts
    cols = [pl.ds(i * tile, tile) for i in range(parts)]
    got_mine = fetch([(mine_ref.at[:, c], mine.at[:, c]) for c in cols], mine_sems)
    got_other = fetch([(other_ref.at[:, c], other.at[:, c]) for c in cols], other_sems)
    pick = (ahead_ref[...] == places_ref[...]).astype(f32).astype(bf16)
    for i, c in enumerate(cols):
        got_mine[i].wait()
        got_other[i].wait()
        if i == 0:
            got_head = fetch([(head_ref.at[c], head.at[c]) for c in cols], head_sems)
        rows = jnp.dot(pick[:, :half], mine[:, c], preferred_element_type=f32)
        rows += jnp.dot(pick[:, half:], other[:, c], preferred_element_type=f32)
        chosen[:, c] = rows.astype(bf16)
    for copy in got_head:
        copy.wait()
    write_product(acc, chosen, head)
    write_coded(acc, code_ref, own_ref)


def coded_shapes(rows, cols):
    return [
        jax.ShapeDtypeStruct((3, rows + TAIL, cols), i16),
        jax.ShapeDtypeStruct((rows, cols), f32),
    ]


def teacher_part(ahead, places, mine, other, head):
    tokens, (half, width), cols = ahead.shape[0], mine.shape, head.shape[1]
    parts = 4
    return pl.pallas_call(
        teacher_kernel,
        in_specs=in_vmem(2) + in_hbm(3),
        out_specs=in_vmem(2),
        out_shape=coded_shapes(tokens // 4, cols),
        scratch_shapes=[
            pltpu.VMEM((half, width), bf16),
            pltpu.VMEM((half, width), bf16),
            pltpu.VMEM((width, cols), bf16),
            pltpu.VMEM((tokens, width), bf16),
            pltpu.VMEM((tokens, cols), f32),
            pltpu.SemaphoreType.DMA((parts,)),
            pltpu.SemaphoreType.DMA((parts,)),
            pltpu.SemaphoreType.DMA((parts,)),
        ],
        compiler_params=pltpu.CompilerParams(vmem_limit_bytes=VMEM),
        cost_estimate=pl.CostEstimate(
            flops=2 * tokens * width * (cols + tokens),
            bytes_accessed=2 * width * (cols + tokens),
            transcendentals=0,
        ),
        name="teacher_part",
    )(ahead[:, None], places[None, :], stay(mine), stay(other), stay(head))


def student_kernel(
    order_ref, mine_ref, other_ref, head_ref, code_ref, own_ref, hidden, head, acc, head_sems
):
    blocks, _, feats = mine_ref.shape
    parts = head_sems.shape[0]
    tile = head.shape[0] // parts
    spans = [pl.ds(i * tile, tile) for i in range(parts)]
    copies = fetch([(head_ref.at[span], head.at[span]) for span in spans], head_sems)
    for i in range(2 * blocks):
        at = pl.multiple_of(order_ref[i] * feats, feats)
        source = mine_ref if i < blocks else other_ref
        hidden[:, pl.ds(at, feats)] = source[i % blocks]
    for copy in copies:
        copy.wait()
    write_product(acc, hidden, head)
    write_coded(acc, code_ref, own_ref)


def student_part(order, mine, other, head):
    (blocks, tokens, feats), (width, cols) = mine.shape, head.shape
    parts = 4
    return pl.pallas_call(
        student_kernel,
        in_specs=[pl.BlockSpec(memory_space=pltpu.SMEM)] + in_vmem(2) + in_hbm(1),
        out_specs=in_vmem(2),
        out_shape=coded_shapes(tokens // 4, cols),
        scratch_shapes=[
            pltpu.VMEM((tokens, width), bf16),
            pltpu.VMEM((width, cols), bf16),
            pltpu.VMEM((tokens, cols), f32),
            pltpu.SemaphoreType.DMA((parts,)),
        ],
        compiler_params=pltpu.CompilerParams(vmem_limit_bytes=VMEM),
        cost_estimate=pl.CostEstimate(
            flops=2 * tokens * width * cols,
            bytes_accessed=2 * width * (cols + tokens),
            transcendentals=0,
        ),
        name="student_part",
    )(order, mine, other, stay(head))


def gradient_kernel(
    where_ref, own_ref, front_ref, far0_ref, far1_ref, behind_ref, head_ref, out_ref,
    delta,
):
    rows, feats = out_ref.shape[3:]
    half = rows // 2
    core, x, y = where_ref[0], where_ref[1], where_ref[2]

    def put(ahead, start, source):
        at = pl.multiple_of(lax.rem(y + ahead, NY) * rows + start, half)
        delta[pl.ds(at, source.shape[0]), :] = source[...]

    put(0, 0, own_ref)
    put(1, 0, front_ref)
    put(2, 0, far0_ref)
    put(2, half, far1_ref)
    put(3, 0, behind_ref)
    for i in range(4):
        span = pl.ds(pl.multiple_of((2 * i + core) * 2 * feats, 2 * feats), 2 * feats)
        grad = lax.dot_general(
            delta[...], head_ref[span, :], (((1,), (1,)), ((), ())), preferred_element_type=f32
        ).astype(out_ref.dtype)
        for xl in range(2):
            ahead = lax.rem(2 * (i % 2) + xl + NX - x, NX)
            for a in range(4):
                out_ref[ahead, a, i // 2] = grad[
                    a * rows : (a + 1) * rows, xl * feats : (xl + 1) * feats
                ]


def gradient_part(core, x, y, pieces, head, dtype):
    (rows, cols), width = pieces[0].shape, head.shape[0]
    tokens, feats = 4 * rows, width // 16
    return pl.pallas_call(
        gradient_kernel,
        in_specs=[pl.BlockSpec(memory_space=pltpu.SMEM)] + in_vmem(len(pieces) + 1),
        out_specs=in_vmem(1)[0],
        scratch_shapes=[
            pltpu.VMEM((tokens, cols), bf16),
        ],
        out_shape=jax.ShapeDtypeStruct((4, 4, 2, rows, feats), dtype),
        compiler_params=pltpu.CompilerParams(vmem_limit_bytes=VMEM),
        cost_estimate=pl.CostEstimate(
            flops=tokens * width * cols,
            bytes_accessed=width * cols + 2 * tokens * cols,
            transcendentals=0,
        ),
        name="gradient_part",
    )(jnp.stack([core, x, y]).astype(jnp.int32), *pieces, keep(head))


def send_coded(code):
    return [shift(code[k - 1], "y", NY, k) for k in (2, 1, 3)]


def finish_sum(own, received):
    rows = own.shape[0]
    out = own
    for got in received:
        scale = jnp.exp2(got[rows, :rows].astype(f32)) * (1.0 / TOP)
        out = out + got[:rows].astype(f32) * scale[:, None]
    return out


def per_device(
    teacher_hidden,
    teacher_head,
    student_hidden,
    student_head,
    teacher_rest,
    student_rest,
    sampled,
    assign,
):
    y, zh, zl = lax.axis_index("y"), lax.axis_index("zh"), lax.axis_index("zl")
    x, c = lax.axis_index(X), lax.axis_index("c")
    tok_rows, feats = student_hidden.shape
    vocab_cols = student_head.shape[1]
    ahead = lax.dynamic_slice_in_dim(
        jnp.concatenate([assign, assign]), y * tok_rows, 4 * tok_rows, 0
    )
    xs = (x - jnp.arange(NX)) % NX

    n = teacher_hidden.shape[0]
    rows = jnp.concatenate(
        [teacher_hidden] + [shift(teacher_hidden, X, NX, k) for k in range(1, NX)], 0
    )
    rows, student_hidden = lax.optimization_barrier((rows, student_hidden))
    rows = lax.all_gather(rows, Z, axis=0, tiled=True)

    token_ids = jnp.take(sampled, ahead[:tok_rows], axis=0)

    got = jnp.stack(
        [lax.ppermute(student_hidden, ("y", "zh"), swap_pairs(k)) for k in range(4)][::-1]
    )
    got = turn(got, 3 - (zh - y) % 4, 4).reshape(4 * tok_rows, feats)
    got = jnp.stack([got, lax.ppermute(got, "zl", [(0, 1), (1, 0)])])
    got = [got] + [shift(got, X, NX, k) for k in (2, 1, 3)]
    got_other = jnp.concatenate([other_core(g) for g in got], 0)
    got = jnp.concatenate(got, 0)
    xo = (x - jnp.array([0, 2, 1, 3])) % NX
    quarter = jnp.stack([zl, 1 - zl])[None, :] * 8 + (xo // 2 * 4 + xo % 2)[:, None]
    order = (quarter[None] + jnp.stack([c, 1 - c])[:, None, None] * 2).reshape(-1)
    rows, got_other = lax.optimization_barrier((rows, got_other))
    student_code, student_own = student_part(order, got, got_other, student_head)

    student_got = send_coded(student_code)
    rows_other = other_core(rows)
    z_places = jnp.arange(NZ)[:, None] * 8 + (xs // 2 * 4 + xs % 2)[None, :]
    places = jnp.stack([z_places + 2 * c, z_places + 2 * (1 - c)])[..., None] * n + jnp.arange(n)
    teacher_code, teacher_own = teacher_part(
        ahead, places.reshape(-1), rows, rows_other, teacher_head
    )
    student_got, teacher_got = lax.optimization_barrier((student_got, send_coded(teacher_code)))
    student_logit = finish_sum(student_own, student_got)
    teacher_logit = finish_sum(teacher_own, teacher_got)

    col_index = lax.axis_index(VOCAB) * vocab_cols + lax.broadcasted_iota(
        jnp.int32, (1, vocab_cols), 1
    )
    teacher_exp = jnp.exp(teacher_logit - teacher_rest[:, None])
    student_exp = jnp.exp(student_logit - student_rest[:, None])
    sums = jnp.stack(
        [
            jnp.sum(teacher_exp, axis=1),
            jnp.sum(student_exp, axis=1),
            jnp.sum(teacher_exp * (teacher_logit - student_logit), axis=1),
            jnp.sum(jnp.where(col_index == token_ids[:, None], student_logit, 0.0), axis=1),
        ]
    )
    sums = lax.all_to_all(jnp.broadcast_to(sums[None], (64,) + sums.shape), VOCAB, 0, 0)
    teacher_total, student_total, gap, picked = jnp.sum(sums, axis=0)
    teacher_norm = teacher_rest + jnp.log(1.0 + teacher_total)
    student_norm = student_rest + jnp.log(1.0 + student_total)
    teacher_scale = 1.0 / (1.0 + teacher_total)
    student_scale = 1.0 / (1.0 + student_total)
    divergence = (gap - (teacher_norm - student_norm) * teacher_total) * teacher_scale
    sampled_logprob = picked - student_norm

    delta = (
        loss_scale * (student_exp * student_scale[:, None] - teacher_exp * teacher_scale[:, None])
    ).astype(bf16)
    half = tok_rows // 2
    behind = shift(delta, "y", NY, 1)
    front = shift(delta, "y", NY, -1)
    far = [shift(behind[:half], "y", NY, 1), shift(front[half:], "y", NY, -1)]
    pieces = [delta, front] + far + [behind]

    theirs = other_core(gradient_part(1 - c, x, y, pieces, student_head, bf16))
    mine = gradient_part(c, x, y, pieces, student_head, f32)
    both = mine + theirs.astype(f32)
    grad = both[0]
    for k in (2, 1, 3):
        grad = grad + shift(both[k].astype(bf16), X, NX, k).astype(f32)
    grad = lax.all_to_all(grad.astype(bf16).reshape(NZ, tok_rows, feats), Z, 0, 0)
    grad = jnp.sum(grad.astype(f32), axis=0).astype(bf16)
    hidden_grad = lax.ppermute(grad, ("y", "zh"), swap_pairs(0))
    return (hidden_grad, divergence, sampled_logprob)


def solution(mesh):
    fine = Mesh(np.asarray(mesh.devices).reshape(SIZES), AXES)
    return jax.shard_map(
        per_device,
        mesh=fine,
        in_specs=(
            P(VOCAB, "y"),
            P("y", VOCAB),
            P("y", VOCAB),
            P("y", VOCAB),
            P("y"),
            P("y"),
            P(),
            P(),
        ),
        out_specs=(P("y", VOCAB), P("y"), P("y")),
        check_vma=False,
    )
```

```python
import jax
import jax.numpy as jnp
import numpy as np
from jax import lax
from jax.experimental import pallas as pl
from jax.experimental.pallas import tpu as pltpu
from jax.sharding import Mesh, PartitionSpec as P

loss_scale = 256.0
f32, bf16, i16 = jnp.float32, jnp.bfloat16, jnp.int16

AXES = ("y", "zh", "zl", "xh", "c", "xl")
SIZES = (4, 4, 2, 2, 2, 2)
X = ("xh", "xl")
Z = ("zh", "zl")
VOCAB = ("zh", "zl", "xh", "c", "xl")
NY, NX, NZ = 4, 4, 8
TAIL = 16
TOP = 32766.0
VMEM = 40 * 1024 * 1024


def shift(a, axes, n, k):
    return lax.ppermute(a, axes, [(i, (i + k) % n) for i in range(n)])


def other_core(a):
    return lax.ppermute(a, "c", [(0, 1), (1, 0)])


def turn(a, start, n):
    return lax.dynamic_slice_in_dim(jnp.concatenate([a, a], 0), start, n, 0)


def swap_pairs(k):
    return [(s * 4 + t, t * 4 + (s + k) % 4) for s in range(4) for t in range(4)]


def write_coded(part_ref, code_ref, own_ref):
    rows, cols = own_ref.shape
    own_ref[...] = part_ref[:rows, :]
    diagonal = lax.broadcasted_iota(jnp.int32, (rows, rows), 0) == lax.broadcasted_iota(
        jnp.int32, (rows, rows), 1
    )
    for b in range(1, 4):
        part = part_ref[b * rows : (b + 1) * rows, :]
        top = jnp.max(jnp.abs(part), axis=1, keepdims=True)
        power = jnp.ceil(jnp.log(jnp.maximum(top, 1e-30)) * 1.4426950408889634 + 0.001)
        power = jnp.clip(power, -90.0, 126.0)
        code = jnp.floor(part * (jnp.exp(power * -0.6931471805599453) * TOP) + 0.5)
        code = jnp.clip(code, -32767.0, 32767.0)
        code_ref[b - 1, :rows, :] = code.astype(jnp.int32).astype(i16)
        across = jnp.sum(jnp.where(diagonal, power, 0.0), axis=0, keepdims=True)
        across = jnp.broadcast_to(across, (TAIL, rows))
        code_ref[b - 1, rows:, :rows] = across.astype(jnp.int32).astype(i16)
        if cols > rows:
            code_ref[b - 1, rows:, rows:] = jnp.zeros((TAIL, cols - rows), i16)


def in_hbm(n):
    return [pl.BlockSpec(memory_space=pltpu.HBM)] * n


def in_vmem(n):
    return [pl.BlockSpec(memory_space=pltpu.VMEM)] * n


def stay(a):
    return pltpu.with_memory_space_constraint(a, pltpu.HBM)


def keep(a):
    return pltpu.with_memory_space_constraint(a, pltpu.VMEM)


def fetch(pairs, sems):
    copies = [pltpu.make_async_copy(a, b, sems.at[i]) for i, (a, b) in enumerate(pairs)]
    for copy in copies:
        copy.start()
    return copies


def add_products(acc, source, head, copies):
    tile = head.shape[0] // len(copies)
    for i, copy in enumerate(copies):
        copy.wait()
        if i % 2:
            span = slice((i - 1) * tile, (i + 1) * tile)
            part = jnp.dot(source[:, span], head[span, :], preferred_element_type=f32)
            acc[...] = part if i == 1 else acc[...] + part


def teacher_kernel(
    ahead_ref, places_ref, mine_ref, other_ref, head_ref, code_ref, own_ref,
    mine, head, chosen, acc, mine_sems, head_sems,
):
    half, width = mine_ref.shape
    parts = head_sems.shape[0]
    tile = width // parts
    spans = [pl.ds(i * tile, tile) for i in range(parts)]
    got_mine = fetch([(mine_ref.at[:, span], mine.at[:, span]) for span in spans], mine_sems)
    copies = fetch([(head_ref.at[span], head.at[span]) for span in spans], head_sems)
    pick = (ahead_ref[...] == places_ref[...]).astype(f32).astype(bf16)

    for copy in got_mine:
        copy.wait()

    @pl.loop(0, parts)
    def _(i):
        span = pl.ds(pl.multiple_of(i * tile, tile), tile)
        rows = jnp.dot(pick[:, :half], mine[:, span], preferred_element_type=f32)
        rows += jnp.dot(pick[:, half:], other_ref[:, span], preferred_element_type=f32)
        chosen[:, span] = rows.astype(bf16)

    add_products(acc, chosen, head, copies)
    write_coded(acc, code_ref, own_ref)


def coded_shapes(rows, cols):
    return [
        jax.ShapeDtypeStruct((3, rows + TAIL, cols), i16),
        jax.ShapeDtypeStruct((rows, cols), f32),
    ]


def teacher_part(ahead, places, mine, other, head):
    tokens, (half, width), cols = ahead.shape[0], mine.shape, head.shape[1]
    parts = 4
    return pl.pallas_call(
        teacher_kernel,
        in_specs=in_vmem(2) + in_hbm(1) + in_vmem(1) + in_hbm(1),
        out_specs=in_vmem(2),
        out_shape=coded_shapes(tokens // 4, cols),
        scratch_shapes=[
            pltpu.VMEM((half, width), bf16),
            pltpu.VMEM((width, cols), bf16),
            pltpu.VMEM((tokens, width), bf16),
            pltpu.VMEM((tokens, cols), f32),
            pltpu.SemaphoreType.DMA((parts,)),
            pltpu.SemaphoreType.DMA((parts,)),
        ],
        compiler_params=pltpu.CompilerParams(vmem_limit_bytes=VMEM),
        cost_estimate=pl.CostEstimate(
            flops=2 * tokens * width * (cols + tokens),
            bytes_accessed=2 * width * (cols + tokens),
            transcendentals=0,
        ),
        name="teacher_part",
    )(ahead[:, None], places[None, :], stay(mine), other, stay(head))


def student_kernel(
    order_ref, mine_ref, other_ref, head_ref, code_ref, own_ref, hidden, head, acc, head_sems
):
    blocks, _, feats = mine_ref.shape
    parts = head_sems.shape[0]
    tile = head.shape[0] // parts
    spans = [pl.ds(i * tile, tile) for i in range(parts)]
    copies = fetch([(head_ref.at[span], head.at[span]) for span in spans], head_sems)
    for i in range(2 * blocks):
        at = pl.multiple_of(order_ref[i] * feats, feats)
        source = mine_ref if i < blocks else other_ref
        hidden[:, pl.ds(at, feats)] = source[i % blocks]
    add_products(acc, hidden, head, copies)
    write_coded(acc, code_ref, own_ref)


def student_part(order, mine, other, head):
    (blocks, tokens, feats), (width, cols) = mine.shape, head.shape
    parts = 4
    return pl.pallas_call(
        student_kernel,
        in_specs=[pl.BlockSpec(memory_space=pltpu.SMEM)] + in_vmem(2) + in_hbm(1),
        out_specs=in_vmem(2),
        out_shape=coded_shapes(tokens // 4, cols),
        scratch_shapes=[
            pltpu.VMEM((tokens, width), bf16),
            pltpu.VMEM((width, cols), bf16),
            pltpu.VMEM((tokens, cols), f32),
            pltpu.SemaphoreType.DMA((parts,)),
        ],
        compiler_params=pltpu.CompilerParams(vmem_limit_bytes=VMEM),
        cost_estimate=pl.CostEstimate(
            flops=2 * tokens * width * cols,
            bytes_accessed=2 * width * (cols + tokens),
            transcendentals=0,
        ),
        name="student_part",
    )(order, mine, other, stay(head))


def gradient_kernel(
    where_ref, own_ref, front_ref, far0_ref, far1_ref, behind_ref, head_ref, out_ref,
    delta,
):
    rows, feats = out_ref.shape[3:]
    half = rows // 2
    core, x, y = where_ref[0], where_ref[1], where_ref[2]

    def put(ahead, start, source):
        at = pl.multiple_of(lax.rem(y + ahead, NY) * rows + start, half)
        delta[pl.ds(at, source.shape[0]), :] = source[...]

    put(0, 0, own_ref)
    put(1, 0, front_ref)
    put(2, 0, far0_ref)
    put(2, half, far1_ref)
    put(3, 0, behind_ref)
    for i in range(4):
        span = pl.ds(pl.multiple_of((2 * i + core) * 2 * feats, 2 * feats), 2 * feats)
        grad = lax.dot_general(
            delta[...], head_ref[span, :], (((1,), (1,)), ((), ())), preferred_element_type=f32
        ).astype(out_ref.dtype)
        for xl in range(2):
            ahead = lax.rem(2 * (i % 2) + xl + NX - x, NX)
            for a in range(4):
                out_ref[ahead, a, i // 2] = grad[
                    a * rows : (a + 1) * rows, xl * feats : (xl + 1) * feats
                ]


def gradient_part(core, x, y, pieces, head, dtype):
    (rows, cols), width = pieces[0].shape, head.shape[0]
    tokens, feats = 4 * rows, width // 16
    return pl.pallas_call(
        gradient_kernel,
        in_specs=[pl.BlockSpec(memory_space=pltpu.SMEM)] + in_vmem(len(pieces) + 1),
        out_specs=in_vmem(1)[0],
        scratch_shapes=[
            pltpu.VMEM((tokens, cols), bf16),
        ],
        out_shape=jax.ShapeDtypeStruct((4, 4, 2, rows, feats), dtype),
        compiler_params=pltpu.CompilerParams(vmem_limit_bytes=VMEM),
        cost_estimate=pl.CostEstimate(
            flops=tokens * width * cols,
            bytes_accessed=width * cols + 2 * tokens * cols,
            transcendentals=0,
        ),
        name="gradient_part",
    )(jnp.stack([core, x, y]).astype(jnp.int32), *pieces, keep(head))


def send_coded(code):
    return [shift(code[k - 1], "y", NY, k) for k in (2, 1, 3)]


def finish_sum(own, received):
    rows = own.shape[0]
    out = own
    for got in received:
        scale = jnp.exp2(got[rows, :rows].astype(f32)) * (1.0 / TOP)
        out = out + got[:rows].astype(f32) * scale[:, None]
    return out


def finish_kernel(got0_ref, got1_ref, got2_ref, own_ref, other_ref, rest_ref, exp_ref, sums_ref):
    rows = own_ref.shape[0]
    diagonal = lax.broadcasted_iota(jnp.int32, (rows, rows), 0) == lax.broadcasted_iota(
        jnp.int32, (rows, rows), 1
    )

    def upright(line):
        return jnp.sum(jnp.where(diagonal, line, 0.0), axis=1, keepdims=True)

    def lying(column):
        return jnp.sum(jnp.where(diagonal, column, 0.0), axis=0, keepdims=True)

    logit = own_ref[...]
    for got in (got0_ref, got1_ref, got2_ref):
        power = upright(got[rows:, :rows].astype(jnp.int32).astype(f32)[:1])
        scale = jnp.exp(power * 0.6931471805599453) * (1.0 / TOP)
        logit = logit + got[:rows, :].astype(jnp.int32).astype(f32) * scale
    exps = jnp.exp(logit - upright(rest_ref[...]))
    exp_ref[...] = exps
    sums_ref[:1, :] = lying(jnp.sum(exps, axis=1, keepdims=True))
    sums_ref[1:, :] = lying(jnp.sum(exps * (logit - other_ref[...]), axis=1, keepdims=True))


def finish_teacher(got, own, student_logit, rest):
    rows, cols = own.shape
    return pl.pallas_call(
        finish_kernel,
        in_specs=in_vmem(6),
        out_specs=in_vmem(2),
        out_shape=[jax.ShapeDtypeStruct((rows, cols), f32), jax.ShapeDtypeStruct((2, rows), f32)],
        compiler_params=pltpu.CompilerParams(vmem_limit_bytes=VMEM),
        cost_estimate=pl.CostEstimate(
            flops=20 * rows * cols, bytes_accessed=18 * rows * cols, transcendentals=rows * cols
        ),
        name="finish_teacher",
    )(*got, own, student_logit, rest[None, :])


def per_device(
    teacher_hidden,
    teacher_head,
    student_hidden,
    student_head,
    teacher_rest,
    student_rest,
    sampled,
    assign,
):
    y, zh, zl = lax.axis_index("y"), lax.axis_index("zh"), lax.axis_index("zl")
    x, c = lax.axis_index(X), lax.axis_index("c")
    tok_rows, feats = student_hidden.shape
    vocab_cols = student_head.shape[1]
    ahead = lax.dynamic_slice_in_dim(
        jnp.concatenate([assign, assign]), y * tok_rows, 4 * tok_rows, 0
    )
    xs = (x - jnp.arange(NX)) % NX

    n = teacher_hidden.shape[0]
    rows = [teacher_hidden] + [shift(teacher_hidden, X, NX, k) for k in range(1, NX)]
    mate = lax.ppermute(student_hidden, "zl", [(0, 1), (1, 0)])
    rows = jnp.concatenate(rows, 0)
    rows, student_hidden, mate = lax.optimization_barrier((rows, student_hidden, mate))
    rows = lax.all_gather(rows, Z, axis=0, tiled=True)

    got = jnp.stack([student_hidden, mate])
    got = jnp.stack([lax.ppermute(got, ("y", "zh"), swap_pairs(k)) for k in range(4)][::-1])
    got = turn(got, 3 - (zh - y) % 4, 4).transpose(1, 0, 2, 3).reshape(2, 4 * tok_rows, feats)
    got = [got] + [shift(got, X, NX, k) for k in (2, 1, 3)]
    got_other = jnp.concatenate([other_core(g) for g in got], 0)
    got = jnp.concatenate(got, 0)
    xo = (x - jnp.array([0, 2, 1, 3])) % NX
    quarter = jnp.stack([zl, 1 - zl])[None, :] * 8 + (xo // 2 * 4 + xo % 2)[:, None]
    order = (quarter[None] + jnp.stack([c, 1 - c])[:, None, None] * 2).reshape(-1)
    student_code, student_own = student_part(order, got, got_other, student_head)

    rows, student_code = lax.optimization_barrier((rows, student_code))
    student_got = send_coded(student_code)
    rows_other = other_core(rows)
    z_places = jnp.arange(NZ)[:, None] * 8 + (xs // 2 * 4 + xs % 2)[None, :]
    places = jnp.stack([z_places + 2 * c, z_places + 2 * (1 - c)])[..., None] * n + jnp.arange(n)
    teacher_code, teacher_own = teacher_part(
        ahead, places.reshape(-1), rows, rows_other, teacher_head
    )
    student_got, teacher_code = lax.optimization_barrier((student_got, teacher_code))
    student_logit = finish_sum(student_own, student_got)

    position = lax.broadcasted_iota(jnp.int32, (1, sampled.shape[0]), 1)
    token_ids = jnp.sum(
        jnp.where(ahead[:tok_rows, None] == position, sampled[None, :], 0), axis=1
    )
    col_index = lax.axis_index(VOCAB) * vocab_cols + lax.broadcasted_iota(
        jnp.int32, (1, vocab_cols), 1
    )
    student_exp = jnp.exp(student_logit - student_rest[:, None])
    student_sums = jnp.stack(
        [
            jnp.sum(student_exp, axis=1),
            jnp.sum(jnp.where(col_index == token_ids[:, None], student_logit, 0.0), axis=1),
        ]
    )
    teacher_exp, teacher_sums = finish_teacher(
        send_coded(teacher_code), teacher_own, student_logit, teacher_rest
    )
    sums = jnp.concatenate([teacher_sums, student_sums], 0)
    sums = lax.all_to_all(jnp.broadcast_to(sums[None], (64,) + sums.shape), VOCAB, 0, 0)
    teacher_total, gap, student_total, picked = jnp.sum(sums, axis=0)
    teacher_norm = teacher_rest + jnp.log(1.0 + teacher_total)
    student_norm = student_rest + jnp.log(1.0 + student_total)
    teacher_scale = 1.0 / (1.0 + teacher_total)
    student_scale = 1.0 / (1.0 + student_total)
    divergence = (gap - (teacher_norm - student_norm) * teacher_total) * teacher_scale
    sampled_logprob = picked - student_norm

    delta = (
        loss_scale * (student_exp * student_scale[:, None] - teacher_exp * teacher_scale[:, None])
    ).astype(bf16)
    half = tok_rows // 2
    behind = shift(delta, "y", NY, 1)
    front = shift(delta, "y", NY, -1)
    far = [shift(behind[:half], "y", NY, 1), shift(front[half:], "y", NY, -1)]
    pieces = [delta, front] + far + [behind]

    theirs = other_core(gradient_part(1 - c, x, y, pieces, student_head, bf16))
    mine = gradient_part(c, x, y, pieces, student_head, f32)
    both = mine + theirs.astype(f32)
    grad = both[0]
    for k in (2, 1, 3):
        grad = grad + shift(both[k].astype(bf16), X, NX, k).astype(f32)
    grad = lax.all_to_all(grad.astype(bf16).reshape(NZ, tok_rows, feats), Z, 0, 0)
    grad = jnp.sum(grad.astype(f32), axis=0).astype(bf16)
    hidden_grad = lax.ppermute(grad, ("y", "zh"), swap_pairs(0))
    return (hidden_grad, divergence, sampled_logprob)


def solution(mesh):
    fine = Mesh(np.asarray(mesh.devices).reshape(SIZES), AXES)
    return jax.shard_map(
        per_device,
        mesh=fine,
        in_specs=(
            P(VOCAB, "y"),
            P("y", VOCAB),
            P("y", VOCAB),
            P("y", VOCAB),
            P("y"),
            P("y"),
            P(),
            P(),
        ),
        out_specs=(P("y", VOCAB), P("y"), P("y")),
        check_vma=False,
    )
```

```python
import jax
import jax.numpy as jnp
import numpy as np
from jax import lax
from jax.experimental import pallas as pl
from jax.experimental.pallas import tpu as pltpu
from jax.sharding import Mesh, PartitionSpec as P

loss_scale = 256.0
f32, bf16, i16 = jnp.float32, jnp.bfloat16, jnp.int16

AXES = ("y", "zh", "zl", "xh", "c", "xl")
SIZES = (4, 4, 2, 2, 2, 2)
X = ("xh", "xl")
Z = ("zh", "zl")
VOCAB = ("zh", "zl", "xh", "c", "xl")
NY, NX, NZ = 4, 4, 8
TAIL = 16
TOP = 32766.0
VMEM = 40 * 1024 * 1024


def shift(a, axes, n, k):
    return lax.ppermute(a, axes, [(i, (i + k) % n) for i in range(n)])


def other_core(a):
    return lax.ppermute(a, "c", [(0, 1), (1, 0)])


def turn(a, start, n):
    return lax.dynamic_slice_in_dim(jnp.concatenate([a, a], 0), start, n, 0)


def swap_pairs(k):
    return [(s * 4 + t, t * 4 + (s + k) % 4) for s in range(4) for t in range(4)]


def write_coded(part_ref, code_ref, own_ref):
    rows, cols = own_ref.shape
    own_ref[...] = part_ref[:rows, :]
    diagonal = lax.broadcasted_iota(jnp.int32, (rows, rows), 0) == lax.broadcasted_iota(
        jnp.int32, (rows, rows), 1
    )
    for b in range(1, 4):
        part = part_ref[b * rows : (b + 1) * rows, :]
        top = jnp.max(jnp.abs(part), axis=1, keepdims=True)
        power = jnp.ceil(jnp.log(jnp.maximum(top, 1e-30)) * 1.4426950408889634 + 0.001)
        power = jnp.clip(power, -90.0, 126.0)
        code = jnp.floor(part * (jnp.exp(power * -0.6931471805599453) * TOP) + 0.5)
        code = jnp.clip(code, -32767.0, 32767.0)
        code_ref[b - 1, :rows, :] = code.astype(jnp.int32).astype(i16)
        across = jnp.sum(jnp.where(diagonal, power, 0.0), axis=0, keepdims=True)
        across = jnp.broadcast_to(across, (TAIL, rows))
        code_ref[b - 1, rows:, :rows] = across.astype(jnp.int32).astype(i16)
        if cols > rows:
            code_ref[b - 1, rows:, rows:] = jnp.zeros((TAIL, cols - rows), i16)


def in_hbm(n):
    return [pl.BlockSpec(memory_space=pltpu.HBM)] * n


def in_vmem(n):
    return [pl.BlockSpec(memory_space=pltpu.VMEM)] * n


def stay(a):
    return pltpu.with_memory_space_constraint(a, pltpu.HBM)


def keep(a):
    return pltpu.with_memory_space_constraint(a, pltpu.VMEM)


def fetch(pairs, sems):
    copies = [pltpu.make_async_copy(a, b, sems.at[i]) for i, (a, b) in enumerate(pairs)]
    for copy in copies:
        copy.start()
    return copies


def add_products(acc, source, head, copies):
    tile = head.shape[0] // len(copies)
    for i, copy in enumerate(copies):
        copy.wait()
        if i % 2:
            span = slice((i - 1) * tile, (i + 1) * tile)
            part = jnp.dot(source[:, span], head[span, :], preferred_element_type=f32)
            acc[...] = part if i == 1 else acc[...] + part


def teacher_kernel(
    ahead_ref, places_ref, mine_ref, other_ref, head_ref, code_ref, own_ref,
    mine, other, head, chosen, acc, mine_sems, other_sems, head_sems,
):
    half, width = mine_ref.shape
    parts = head_sems.shape[0]
    tile = width // parts
    spans = [pl.ds(i * tile, tile) for i in range(parts)]
    got_mine = fetch([(mine_ref.at[:, span], mine.at[:, span]) for span in spans], mine_sems)
    got_other = fetch([(other_ref.at[:, span], other.at[:, span]) for span in spans], other_sems)
    pick = (ahead_ref[...] == places_ref[...]).astype(f32).astype(bf16)
    for i, span in enumerate(spans):
        got_mine[i].wait()
        got_other[i].wait()
        if i == 0:
            copies = fetch([(head_ref.at[span], head.at[span]) for span in spans], head_sems)
        rows = jnp.dot(pick[:, :half], mine[:, span], preferred_element_type=f32)
        rows += jnp.dot(pick[:, half:], other[:, span], preferred_element_type=f32)
        chosen[:, span] = rows.astype(bf16)
    add_products(acc, chosen, head, copies)
    write_coded(acc, code_ref, own_ref)


def coded_shapes(rows, cols):
    return [
        jax.ShapeDtypeStruct((3, rows + TAIL, cols), i16),
        jax.ShapeDtypeStruct((rows, cols), f32),
    ]


def teacher_part(ahead, places, mine, other, head):
    tokens, (half, width), cols = ahead.shape[0], mine.shape, head.shape[1]
    parts = 4
    return pl.pallas_call(
        teacher_kernel,
        in_specs=in_vmem(2) + in_hbm(3),
        out_specs=in_vmem(2),
        out_shape=coded_shapes(tokens // 4, cols),
        scratch_shapes=[
            pltpu.VMEM((half, width), bf16),
            pltpu.VMEM((half, width), bf16),
            pltpu.VMEM((width, cols), bf16),
            pltpu.VMEM((tokens, width), bf16),
            pltpu.VMEM((tokens, cols), f32),
            pltpu.SemaphoreType.DMA((parts,)),
            pltpu.SemaphoreType.DMA((parts,)),
            pltpu.SemaphoreType.DMA((parts,)),
        ],
        compiler_params=pltpu.CompilerParams(vmem_limit_bytes=VMEM),
        cost_estimate=pl.CostEstimate(
            flops=2 * tokens * width * (cols + tokens),
            bytes_accessed=2 * width * (cols + tokens),
            transcendentals=0,
        ),
        name="teacher_part",
    )(ahead[:, None], places[None, :], stay(mine), stay(other), stay(head))


def student_kernel(
    order_ref, mine_ref, other_ref, head_ref, code_ref, own_ref, hidden, head, acc, head_sems
):
    blocks, _, feats = mine_ref.shape
    parts = head_sems.shape[0]
    tile = head.shape[0] // parts
    spans = [pl.ds(i * tile, tile) for i in range(parts)]
    copies = fetch([(head_ref.at[span], head.at[span]) for span in spans], head_sems)
    for i in range(2 * blocks):
        at = pl.multiple_of(order_ref[i] * feats, feats)
        source = mine_ref if i < blocks else other_ref
        hidden[:, pl.ds(at, feats)] = source[i % blocks]
    add_products(acc, hidden, head, copies)
    write_coded(acc, code_ref, own_ref)


def student_part(order, mine, other, head):
    (blocks, tokens, feats), (width, cols) = mine.shape, head.shape
    parts = 4
    return pl.pallas_call(
        student_kernel,
        in_specs=[pl.BlockSpec(memory_space=pltpu.SMEM)] + in_vmem(2) + in_hbm(1),
        out_specs=in_vmem(2),
        out_shape=coded_shapes(tokens // 4, cols),
        scratch_shapes=[
            pltpu.VMEM((tokens, width), bf16),
            pltpu.VMEM((width, cols), bf16),
            pltpu.VMEM((tokens, cols), f32),
            pltpu.SemaphoreType.DMA((parts,)),
        ],
        compiler_params=pltpu.CompilerParams(vmem_limit_bytes=VMEM),
        cost_estimate=pl.CostEstimate(
            flops=2 * tokens * width * cols,
            bytes_accessed=2 * width * (cols + tokens),
            transcendentals=0,
        ),
        name="student_part",
    )(order, mine, other, stay(head))


def gradient_kernel(
    where_ref, own_ref, front_ref, far0_ref, far1_ref, behind_ref, head_ref, out_ref,
    delta,
):
    rows, feats = out_ref.shape[3:]
    half = rows // 2
    core, x, y = where_ref[0], where_ref[1], where_ref[2]

    def put(ahead, start, source):
        at = pl.multiple_of(lax.rem(y + ahead, NY) * rows + start, half)
        delta[pl.ds(at, source.shape[0]), :] = source[...]

    put(0, 0, own_ref)
    put(1, 0, front_ref)
    put(2, 0, far0_ref)
    put(2, half, far1_ref)
    put(3, 0, behind_ref)
    for i in range(4):
        span = pl.ds(pl.multiple_of((2 * i + core) * 2 * feats, 2 * feats), 2 * feats)
        grad = lax.dot_general(
            delta[...], head_ref[span, :], (((1,), (1,)), ((), ())), preferred_element_type=f32
        ).astype(out_ref.dtype)
        for xl in range(2):
            ahead = lax.rem(2 * (i % 2) + xl + NX - x, NX)
            for a in range(4):
                out_ref[ahead, a, i // 2] = grad[
                    a * rows : (a + 1) * rows, xl * feats : (xl + 1) * feats
                ]


def gradient_part(core, x, y, pieces, head, dtype):
    (rows, cols), width = pieces[0].shape, head.shape[0]
    tokens, feats = 4 * rows, width // 16
    return pl.pallas_call(
        gradient_kernel,
        in_specs=[pl.BlockSpec(memory_space=pltpu.SMEM)] + in_vmem(len(pieces) + 1),
        out_specs=in_vmem(1)[0],
        scratch_shapes=[
            pltpu.VMEM((tokens, cols), bf16),
        ],
        out_shape=jax.ShapeDtypeStruct((4, 4, 2, rows, feats), dtype),
        compiler_params=pltpu.CompilerParams(vmem_limit_bytes=VMEM),
        cost_estimate=pl.CostEstimate(
            flops=tokens * width * cols,
            bytes_accessed=width * cols + 2 * tokens * cols,
            transcendentals=0,
        ),
        name="gradient_part",
    )(jnp.stack([core, x, y]).astype(jnp.int32), *pieces, keep(head))


def send_coded(code):
    return [shift(code[k - 1], "y", NY, k) for k in (2, 1, 3)]


def finish_sum(own, received):
    rows = own.shape[0]
    out = own
    for got in received:
        scale = jnp.exp2(got[rows, :rows].astype(f32)) * (1.0 / TOP)
        out = out + got[:rows].astype(f32) * scale[:, None]
    return out


def finish_kernel(got0_ref, got1_ref, got2_ref, own_ref, other_ref, rest_ref, exp_ref, sums_ref):
    rows = own_ref.shape[0]
    diagonal = lax.broadcasted_iota(jnp.int32, (rows, rows), 0) == lax.broadcasted_iota(
        jnp.int32, (rows, rows), 1
    )

    def upright(line):
        return jnp.sum(jnp.where(diagonal, line, 0.0), axis=1, keepdims=True)

    def lying(column):
        return jnp.sum(jnp.where(diagonal, column, 0.0), axis=0, keepdims=True)

    logit = own_ref[...]
    for got in (got0_ref, got1_ref, got2_ref):
        power = upright(got[rows:, :rows].astype(jnp.int32).astype(f32)[:1])
        scale = jnp.exp(power * 0.6931471805599453) * (1.0 / TOP)
        logit = logit + got[:rows, :].astype(jnp.int32).astype(f32) * scale
    exps = jnp.exp(logit - upright(rest_ref[...]))
    exp_ref[...] = exps
    sums_ref[:1, :] = lying(jnp.sum(exps, axis=1, keepdims=True))
    sums_ref[1:, :] = lying(jnp.sum(exps * (logit - other_ref[...]), axis=1, keepdims=True))


def finish_teacher(got, own, student_logit, rest):
    rows, cols = own.shape
    return pl.pallas_call(
        finish_kernel,
        in_specs=in_vmem(6),
        out_specs=in_vmem(2),
        out_shape=[jax.ShapeDtypeStruct((rows, cols), f32), jax.ShapeDtypeStruct((2, rows), f32)],
        compiler_params=pltpu.CompilerParams(vmem_limit_bytes=VMEM),
        cost_estimate=pl.CostEstimate(
            flops=20 * rows * cols, bytes_accessed=18 * rows * cols, transcendentals=rows * cols
        ),
        name="finish_teacher",
    )(*got, own, student_logit, rest[None, :])


def per_device(
    teacher_hidden,
    teacher_head,
    student_hidden,
    student_head,
    teacher_rest,
    student_rest,
    sampled,
    assign,
):
    y, zh, zl = lax.axis_index("y"), lax.axis_index("zh"), lax.axis_index("zl")
    x, c = lax.axis_index(X), lax.axis_index("c")
    tok_rows, feats = student_hidden.shape
    vocab_cols = student_head.shape[1]
    ahead = lax.dynamic_slice_in_dim(
        jnp.concatenate([assign, assign]), y * tok_rows, 4 * tok_rows, 0
    )
    xs = (x - jnp.arange(NX)) % NX

    n = teacher_hidden.shape[0]
    rows = [teacher_hidden] + [shift(teacher_hidden, X, NX, k) for k in range(1, NX)]
    mate = lax.ppermute(student_hidden, "zl", [(0, 1), (1, 0)])
    rows = jnp.concatenate(rows, 0)
    rows, student_hidden, mate = lax.optimization_barrier((rows, student_hidden, mate))
    rows = lax.all_gather(rows, Z, axis=0, tiled=True)

    got = jnp.stack([student_hidden, mate])
    got = jnp.stack([lax.ppermute(got, ("y", "zh"), swap_pairs(k)) for k in range(4)][::-1])
    got = turn(got, 3 - (zh - y) % 4, 4).transpose(1, 0, 2, 3).reshape(2, 4 * tok_rows, feats)
    got = [got] + [shift(got, X, NX, k) for k in (2, 1, 3)]
    got_other = jnp.concatenate([other_core(g) for g in got], 0)
    got = jnp.concatenate(got, 0)
    xo = (x - jnp.array([0, 2, 1, 3])) % NX
    quarter = jnp.stack([zl, 1 - zl])[None, :] * 8 + (xo // 2 * 4 + xo % 2)[:, None]
    order = (quarter[None] + jnp.stack([c, 1 - c])[:, None, None] * 2).reshape(-1)
    student_code, student_own = student_part(order, got, got_other, student_head)

    rows, student_code = lax.optimization_barrier((rows, student_code))
    student_got = send_coded(student_code)
    rows_other = other_core(rows)
    z_places = jnp.arange(NZ)[:, None] * 8 + (xs // 2 * 4 + xs % 2)[None, :]
    places = jnp.stack([z_places + 2 * c, z_places + 2 * (1 - c)])[..., None] * n + jnp.arange(n)
    teacher_code, teacher_own = teacher_part(
        ahead, places.reshape(-1), rows, rows_other, teacher_head
    )
    teacher_got = send_coded(teacher_code)
    student_got, teacher_got[0] = lax.optimization_barrier((student_got, teacher_got[0]))
    student_logit = finish_sum(student_own, student_got)

    position = lax.broadcasted_iota(jnp.int32, (1, sampled.shape[0]), 1)
    token_ids = jnp.sum(
        jnp.where(ahead[:tok_rows, None] == position, sampled[None, :], 0), axis=1
    )
    col_index = lax.axis_index(VOCAB) * vocab_cols + lax.broadcasted_iota(
        jnp.int32, (1, vocab_cols), 1
    )
    student_exp = jnp.exp(student_logit - student_rest[:, None])
    student_sums = jnp.stack(
        [
            jnp.sum(student_exp, axis=1),
            jnp.sum(jnp.where(col_index == token_ids[:, None], student_logit, 0.0), axis=1),
        ]
    )
    teacher_exp, teacher_sums = finish_teacher(
        teacher_got, teacher_own, student_logit, teacher_rest
    )
    sums = jnp.concatenate([teacher_sums, student_sums], 0)
    sums = lax.all_to_all(jnp.broadcast_to(sums[None], (64,) + sums.shape), VOCAB, 0, 0)
    teacher_total, gap, student_total, picked = jnp.sum(sums, axis=0)
    teacher_norm = teacher_rest + jnp.log(1.0 + teacher_total)
    student_norm = student_rest + jnp.log(1.0 + student_total)
    teacher_scale = 1.0 / (1.0 + teacher_total)
    student_scale = 1.0 / (1.0 + student_total)
    divergence = (gap - (teacher_norm - student_norm) * teacher_total) * teacher_scale
    sampled_logprob = picked - student_norm

    delta = (
        loss_scale * (student_exp * student_scale[:, None] - teacher_exp * teacher_scale[:, None])
    ).astype(bf16)
    half = tok_rows // 2
    behind = shift(delta, "y", NY, 1)
    front = shift(delta, "y", NY, -1)
    far = [shift(behind[:half], "y", NY, 1), shift(front[half:], "y", NY, -1)]
    pieces = [delta, front] + far + [behind]

    theirs = other_core(gradient_part(1 - c, x, y, pieces, student_head, bf16))
    mine = gradient_part(c, x, y, pieces, student_head, f32)
    both = mine + theirs.astype(f32)
    grad = both[0]
    for k in (2, 1, 3):
        grad = grad + shift(both[k].astype(bf16), X, NX, k).astype(f32)
    grad = lax.all_to_all(grad.astype(bf16).reshape(NZ, tok_rows, feats), Z, 0, 0)
    grad = jnp.sum(grad.astype(f32), axis=0).astype(bf16)
    hidden_grad = lax.ppermute(grad, ("y", "zh"), swap_pairs(0))
    return (hidden_grad, divergence, sampled_logprob)


def solution(mesh):
    fine = Mesh(np.asarray(mesh.devices).reshape(SIZES), AXES)
    return jax.shard_map(
        per_device,
        mesh=fine,
        in_specs=(
            P(VOCAB, "y"),
            P("y", VOCAB),
            P("y", VOCAB),
            P("y", VOCAB),
            P("y"),
            P("y"),
            P(),
            P(),
        ),
        out_specs=(P("y", VOCAB), P("y"), P("y")),
        check_vma=False,
    )
```

```python
import jax
import jax.numpy as jnp
import numpy as np
from jax import lax
from jax.experimental import pallas as pl
from jax.experimental.pallas import tpu as pltpu
from jax.sharding import Mesh, PartitionSpec as P

loss_scale = 256.0
f32, bf16, i16 = jnp.float32, jnp.bfloat16, jnp.int16

AXES = ("y", "zh", "zl", "xh", "c", "xl")
SIZES = (4, 4, 2, 2, 2, 2)
X = ("xh", "xl")
Z = ("zh", "zl")
VOCAB = ("zh", "zl", "xh", "c", "xl")
NY, NX, NZ = 4, 4, 8
TAIL = 16
TOP = 32766.0
VMEM = 40 * 1024 * 1024


def shift(a, axes, n, k):
    return lax.ppermute(a, axes, [(i, (i + k) % n) for i in range(n)])


def other_core(a):
    return lax.ppermute(a, "c", [(0, 1), (1, 0)])


def turn(a, start, n):
    return lax.dynamic_slice_in_dim(jnp.concatenate([a, a], 0), start, n, 0)


def swap_pairs(k):
    return [(s * 4 + t, t * 4 + (s + k) % 4) for s in range(4) for t in range(4)]


def write_coded(part_ref, code_ref, own_ref):
    rows, cols = own_ref.shape
    own_ref[...] = part_ref[:rows, :]
    diagonal = lax.broadcasted_iota(jnp.int32, (rows, rows), 0) == lax.broadcasted_iota(
        jnp.int32, (rows, rows), 1
    )
    for b in range(1, 4):
        part = part_ref[b * rows : (b + 1) * rows, :]
        top = jnp.max(jnp.abs(part), axis=1, keepdims=True)
        power = jnp.ceil(jnp.log(jnp.maximum(top, 1e-30)) * 1.4426950408889634 + 0.001)
        power = jnp.clip(power, -90.0, 126.0)
        code = jnp.floor(part * (jnp.exp(power * -0.6931471805599453) * TOP) + 0.5)
        code = jnp.clip(code, -32767.0, 32767.0)
        code_ref[b - 1, :rows, :] = code.astype(jnp.int32).astype(i16)
        across = jnp.sum(jnp.where(diagonal, power, 0.0), axis=0, keepdims=True)
        across = jnp.broadcast_to(across, (TAIL, rows))
        code_ref[b - 1, rows:, :rows] = across.astype(jnp.int32).astype(i16)
        if cols > rows:
            code_ref[b - 1, rows:, rows:] = jnp.zeros((TAIL, cols - rows), i16)


def in_hbm(n):
    return [pl.BlockSpec(memory_space=pltpu.HBM)] * n


def in_vmem(n):
    return [pl.BlockSpec(memory_space=pltpu.VMEM)] * n


def stay(a):
    return pltpu.with_memory_space_constraint(a, pltpu.HBM)


def keep(a):
    return pltpu.with_memory_space_constraint(a, pltpu.VMEM)


def fetch(pairs, sems):
    copies = [pltpu.make_async_copy(a, b, sems.at[i]) for i, (a, b) in enumerate(pairs)]
    for copy in copies:
        copy.start()
    return copies


def add_products(acc, source, head, copies):
    tile = head.shape[0] // len(copies)
    for i, copy in enumerate(copies):
        copy.wait()
        if i % 2:
            span = slice((i - 1) * tile, (i + 1) * tile)
            part = jnp.dot(source[:, span], head[span, :], preferred_element_type=f32)
            acc[...] = part if i == 1 else acc[...] + part


def teacher_kernel(
    ahead_ref, places_ref, mine_ref, other_ref, head_ref, code_ref, own_ref,
    mine, other, head, chosen, acc, mine_sems, other_sems, head_sems,
):
    half, width = mine_ref.shape
    parts = head_sems.shape[0]
    tile = width // parts
    spans = [pl.ds(i * tile, tile) for i in range(parts)]
    got_mine = fetch([(mine_ref.at[:, span], mine.at[:, span]) for span in spans], mine_sems)
    got_other = fetch([(other_ref.at[:, span], other.at[:, span]) for span in spans], other_sems)
    pick = (ahead_ref[...] == places_ref[...]).astype(f32).astype(bf16)
    for i, span in enumerate(spans):
        got_mine[i].wait()
        got_other[i].wait()
        if i == 0:
            copies = fetch([(head_ref.at[span], head.at[span]) for span in spans], head_sems)
        rows = jnp.dot(pick[:, :half], mine[:, span], preferred_element_type=f32)
        rows += jnp.dot(pick[:, half:], other[:, span], preferred_element_type=f32)
        chosen[:, span] = rows.astype(bf16)
    add_products(acc, chosen, head, copies)
    write_coded(acc, code_ref, own_ref)


def coded_shapes(rows, cols):
    return [
        jax.ShapeDtypeStruct((3, rows + TAIL, cols), i16),
        jax.ShapeDtypeStruct((rows, cols), f32),
    ]


def teacher_part(ahead, places, mine, other, head):
    tokens, (half, width), cols = ahead.shape[0], mine.shape, head.shape[1]
    parts = 4
    return pl.pallas_call(
        teacher_kernel,
        in_specs=in_vmem(2) + in_hbm(3),
        out_specs=in_vmem(2),
        out_shape=coded_shapes(tokens // 4, cols),
        scratch_shapes=[
            pltpu.VMEM((half, width), bf16),
            pltpu.VMEM((half, width), bf16),
            pltpu.VMEM((width, cols), bf16),
            pltpu.VMEM((tokens, width), bf16),
            pltpu.VMEM((tokens, cols), f32),
            pltpu.SemaphoreType.DMA((parts,)),
            pltpu.SemaphoreType.DMA((parts,)),
            pltpu.SemaphoreType.DMA((parts,)),
        ],
        compiler_params=pltpu.CompilerParams(vmem_limit_bytes=VMEM),
        cost_estimate=pl.CostEstimate(
            flops=2 * tokens * width * (cols + tokens),
            bytes_accessed=2 * width * (cols + tokens),
            transcendentals=0,
        ),
        name="teacher_part",
    )(ahead[:, None], places[None, :], stay(mine), stay(other), stay(head))


def student_kernel(
    order_ref, mine_ref, other_ref, head_ref, code_ref, own_ref, hidden, head, acc, head_sems
):
    blocks, _, feats = mine_ref.shape
    parts = head_sems.shape[0]
    tile = head.shape[0] // parts
    spans = [pl.ds(i * tile, tile) for i in range(parts)]
    copies = fetch([(head_ref.at[span], head.at[span]) for span in spans], head_sems)
    for i in range(2 * blocks):
        at = pl.multiple_of(order_ref[i] * feats, feats)
        source = mine_ref if i < blocks else other_ref
        hidden[:, pl.ds(at, feats)] = source[i % blocks]
    add_products(acc, hidden, head, copies)
    write_coded(acc, code_ref, own_ref)


def student_part(order, mine, other, head):
    (blocks, tokens, feats), (width, cols) = mine.shape, head.shape
    parts = 4
    return pl.pallas_call(
        student_kernel,
        in_specs=[pl.BlockSpec(memory_space=pltpu.SMEM)] + in_vmem(2) + in_hbm(1),
        out_specs=in_vmem(2),
        out_shape=coded_shapes(tokens // 4, cols),
        scratch_shapes=[
            pltpu.VMEM((tokens, width), bf16),
            pltpu.VMEM((width, cols), bf16),
            pltpu.VMEM((tokens, cols), f32),
            pltpu.SemaphoreType.DMA((parts,)),
        ],
        compiler_params=pltpu.CompilerParams(vmem_limit_bytes=VMEM),
        cost_estimate=pl.CostEstimate(
            flops=2 * tokens * width * cols,
            bytes_accessed=2 * width * (cols + tokens),
            transcendentals=0,
        ),
        name="student_part",
    )(order, mine, other, stay(head))


def bring_kernel(head_ref, out_ref, sems):
    for copy in fetch([(head_ref, out_ref)], sems):
        copy.wait()


def bring(head):
    return pl.pallas_call(
        bring_kernel,
        in_specs=in_hbm(1),
        out_specs=pl.BlockSpec(memory_space=pl.ANY),
        out_shape=jax.ShapeDtypeStruct(head.shape, head.dtype),
        scratch_shapes=[pltpu.SemaphoreType.DMA((1,))],
        compiler_params=pltpu.CompilerParams(vmem_limit_bytes=1024 * 1024),
        cost_estimate=pl.CostEstimate(
            flops=0, bytes_accessed=4 * head.shape[0] * head.shape[1], transcendentals=0
        ),
        name="bring",
    )(stay(head))


def gradient_kernel(
    where_ref, own_ref, front_ref, far0_ref, far1_ref, behind_ref, head_ref, out_ref,
    delta,
):
    rows, feats = out_ref.shape[3:]
    half = rows // 2
    core, x, y = where_ref[0], where_ref[1], where_ref[2]

    def put(ahead, start, source):
        at = pl.multiple_of(lax.rem(y + ahead, NY) * rows + start, half)
        delta[pl.ds(at, source.shape[0]), :] = source[...]

    put(0, 0, own_ref)
    put(1, 0, front_ref)
    put(2, 0, far0_ref)
    put(2, half, far1_ref)
    put(3, 0, behind_ref)
    for i in range(4):
        span = pl.ds(pl.multiple_of((2 * i + core) * 2 * feats, 2 * feats), 2 * feats)
        grad = lax.dot_general(
            delta[...], head_ref[span, :], (((1,), (1,)), ((), ())), preferred_element_type=f32
        ).astype(out_ref.dtype)
        for xl in range(2):
            ahead = lax.rem(2 * (i % 2) + xl + NX - x, NX)
            for a in range(4):
                out_ref[ahead, a, i // 2] = grad[
                    a * rows : (a + 1) * rows, xl * feats : (xl + 1) * feats
                ]


def gradient_part(core, x, y, pieces, head, dtype):
    (rows, cols), width = pieces[0].shape, head.shape[0]
    tokens, feats = 4 * rows, width // 16
    return pl.pallas_call(
        gradient_kernel,
        in_specs=[pl.BlockSpec(memory_space=pltpu.SMEM)] + in_vmem(len(pieces) + 1),
        out_specs=in_vmem(1)[0],
        scratch_shapes=[
            pltpu.VMEM((tokens, cols), bf16),
        ],
        out_shape=jax.ShapeDtypeStruct((4, 4, 2, rows, feats), dtype),
        compiler_params=pltpu.CompilerParams(vmem_limit_bytes=VMEM),
        cost_estimate=pl.CostEstimate(
            flops=tokens * width * cols,
            bytes_accessed=width * cols + 2 * tokens * cols,
            transcendentals=0,
        ),
        name="gradient_part",
    )(jnp.stack([core, x, y]).astype(jnp.int32), *pieces, keep(head))


def send_coded(code):
    return [shift(code[k - 1], "y", NY, k) for k in (2, 1, 3)]


def finish_sum(own, received):
    rows = own.shape[0]
    out = own
    for got in received:
        scale = jnp.exp2(got[rows, :rows].astype(f32)) * (1.0 / TOP)
        out = out + got[:rows].astype(f32) * scale[:, None]
    return out


def finish_kernel(got0_ref, got1_ref, got2_ref, own_ref, other_ref, rest_ref, exp_ref, sums_ref):
    rows = own_ref.shape[0]
    diagonal = lax.broadcasted_iota(jnp.int32, (rows, rows), 0) == lax.broadcasted_iota(
        jnp.int32, (rows, rows), 1
    )

    def upright(line):
        return jnp.sum(jnp.where(diagonal, line, 0.0), axis=1, keepdims=True)

    def lying(column):
        return jnp.sum(jnp.where(diagonal, column, 0.0), axis=0, keepdims=True)

    logit = own_ref[...]
    for got in (got0_ref, got1_ref, got2_ref):
        power = upright(got[rows:, :rows].astype(jnp.int32).astype(f32)[:1])
        scale = jnp.exp(power * 0.6931471805599453) * (1.0 / TOP)
        logit = logit + got[:rows, :].astype(jnp.int32).astype(f32) * scale
    exps = jnp.exp(logit - upright(rest_ref[...]))
    exp_ref[...] = exps
    sums_ref[:1, :] = lying(jnp.sum(exps, axis=1, keepdims=True))
    sums_ref[1:, :] = lying(jnp.sum(exps * (logit - other_ref[...]), axis=1, keepdims=True))


def finish_teacher(got, own, student_logit, rest):
    rows, cols = own.shape
    return pl.pallas_call(
        finish_kernel,
        in_specs=in_vmem(6),
        out_specs=in_vmem(2),
        out_shape=[jax.ShapeDtypeStruct((rows, cols), f32), jax.ShapeDtypeStruct((2, rows), f32)],
        compiler_params=pltpu.CompilerParams(vmem_limit_bytes=VMEM),
        cost_estimate=pl.CostEstimate(
            flops=20 * rows * cols, bytes_accessed=18 * rows * cols, transcendentals=rows * cols
        ),
        name="finish_teacher",
    )(*got, own, student_logit, rest[None, :])


def per_device(
    teacher_hidden,
    teacher_head,
    student_hidden,
    student_head,
    teacher_rest,
    student_rest,
    sampled,
    assign,
):
    y, zh, zl = lax.axis_index("y"), lax.axis_index("zh"), lax.axis_index("zl")
    x, c = lax.axis_index(X), lax.axis_index("c")
    tok_rows, feats = student_hidden.shape
    vocab_cols = student_head.shape[1]
    ahead = lax.dynamic_slice_in_dim(
        jnp.concatenate([assign, assign]), y * tok_rows, 4 * tok_rows, 0
    )
    xs = (x - jnp.arange(NX)) % NX

    n = teacher_hidden.shape[0]
    rows = [teacher_hidden] + [shift(teacher_hidden, X, NX, k) for k in range(1, NX)]
    mate = lax.ppermute(student_hidden, "zl", [(0, 1), (1, 0)])
    rows = jnp.concatenate(rows, 0)
    rows, student_hidden, mate = lax.optimization_barrier((rows, student_hidden, mate))
    rows = lax.all_gather(rows, Z, axis=0, tiled=True)

    got = jnp.stack([student_hidden, mate])
    got = jnp.stack([lax.ppermute(got, ("y", "zh"), swap_pairs(k)) for k in range(4)][::-1])
    got = turn(got, 3 - (zh - y) % 4, 4).transpose(1, 0, 2, 3).reshape(2, 4 * tok_rows, feats)
    got = [got] + [shift(got, X, NX, k) for k in (2, 1, 3)]
    got_other = jnp.concatenate([other_core(g) for g in got], 0)
    got = jnp.concatenate(got, 0)
    xo = (x - jnp.array([0, 2, 1, 3])) % NX
    quarter = jnp.stack([zl, 1 - zl])[None, :] * 8 + (xo // 2 * 4 + xo % 2)[:, None]
    order = (quarter[None] + jnp.stack([c, 1 - c])[:, None, None] * 2).reshape(-1)
    student_code, student_own = student_part(order, got, got_other, student_head)

    rows, student_code = lax.optimization_barrier((rows, student_code))
    student_got = send_coded(student_code)
    rows_other = other_core(rows)
    z_places = jnp.arange(NZ)[:, None] * 8 + (xs // 2 * 4 + xs % 2)[None, :]
    places = jnp.stack([z_places + 2 * c, z_places + 2 * (1 - c)])[..., None] * n + jnp.arange(n)
    teacher_code, teacher_own = teacher_part(
        ahead, places.reshape(-1), rows, rows_other, teacher_head
    )
    teacher_got = send_coded(teacher_code)
    student_got, teacher_got[0] = lax.optimization_barrier((student_got, teacher_got[0]))
    student_logit = finish_sum(student_own, student_got)

    position = lax.broadcasted_iota(jnp.int32, (1, sampled.shape[0]), 1)
    token_ids = jnp.sum(
        jnp.where(ahead[:tok_rows, None] == position, sampled[None, :], 0), axis=1
    )
    col_index = lax.axis_index(VOCAB) * vocab_cols + lax.broadcasted_iota(
        jnp.int32, (1, vocab_cols), 1
    )
    student_exp = jnp.exp(student_logit - student_rest[:, None])
    student_sums = jnp.stack(
        [
            jnp.sum(student_exp, axis=1),
            jnp.sum(jnp.where(col_index == token_ids[:, None], student_logit, 0.0), axis=1),
        ]
    )
    teacher_exp, teacher_sums = finish_teacher(
        teacher_got, teacher_own, student_logit, teacher_rest
    )
    sums = jnp.concatenate([teacher_sums, student_sums], 0)
    sums = lax.all_to_all(jnp.broadcast_to(sums[None], (64,) + sums.shape), VOCAB, 0, 0)
    teacher_total, gap, student_total, picked = jnp.sum(sums, axis=0)
    teacher_norm = teacher_rest + jnp.log(1.0 + teacher_total)
    student_norm = student_rest + jnp.log(1.0 + student_total)
    teacher_scale = 1.0 / (1.0 + teacher_total)
    student_scale = 1.0 / (1.0 + student_total)
    divergence = (gap - (teacher_norm - student_norm) * teacher_total) * teacher_scale
    sampled_logprob = picked - student_norm

    delta = (
        loss_scale * (student_exp * student_scale[:, None] - teacher_exp * teacher_scale[:, None])
    ).astype(bf16)
    half = tok_rows // 2
    delta, student_head = lax.optimization_barrier((delta, student_head))
    student_head = bring(student_head)
    behind = shift(delta, "y", NY, 1)
    front = shift(delta, "y", NY, -1)
    far = [shift(behind[:half], "y", NY, 1), shift(front[half:], "y", NY, -1)]
    pieces = [delta, front] + far + [behind]

    theirs = other_core(gradient_part(1 - c, x, y, pieces, student_head, bf16))
    mine = gradient_part(c, x, y, pieces, student_head, f32)
    both = mine + theirs.astype(f32)
    grad = both[0]
    for k in (2, 1, 3):
        grad = grad + shift(both[k].astype(bf16), X, NX, k).astype(f32)
    grad = lax.all_to_all(grad.astype(bf16).reshape(NZ, tok_rows, feats), Z, 0, 0)
    grad = jnp.sum(grad.astype(f32), axis=0).astype(bf16)
    hidden_grad = lax.ppermute(grad, ("y", "zh"), swap_pairs(0))
    return (hidden_grad, divergence, sampled_logprob)


def solution(mesh):
    fine = Mesh(np.asarray(mesh.devices).reshape(SIZES), AXES)
    return jax.shard_map(
        per_device,
        mesh=fine,
        in_specs=(
            P(VOCAB, "y"),
            P("y", VOCAB),
            P("y", VOCAB),
            P("y", VOCAB),
            P("y"),
            P("y"),
            P(),
            P(),
        ),
        out_specs=(P("y", VOCAB), P("y"), P("y")),
        check_vma=False,
    )
```

```python
import jax
import jax.numpy as jnp
import numpy as np
from jax import lax
from jax.experimental import pallas as pl
from jax.experimental.pallas import tpu as pltpu
from jax.sharding import Mesh, PartitionSpec as P

loss_scale = 256.0
f32, bf16, i16 = jnp.float32, jnp.bfloat16, jnp.int16

AXES = ("y", "zh", "zl", "xh", "c", "xl")
SIZES = (4, 4, 2, 2, 2, 2)
X = ("xh", "xl")
Z = ("zh", "zl")
VOCAB = ("zh", "zl", "xh", "c", "xl")
NY, NX, NZ = 4, 4, 8
TAIL = 16
TOP = 32766.0
VMEM = 40 * 1024 * 1024


def shift(a, axes, n, k):
    return lax.ppermute(a, axes, [(i, (i + k) % n) for i in range(n)])


def other_core(a):
    return lax.ppermute(a, "c", [(0, 1), (1, 0)])


def turn(a, start, n):
    return lax.dynamic_slice_in_dim(jnp.concatenate([a, a], 0), start, n, 0)


def swap_pairs(k):
    return [(s * 4 + t, t * 4 + (s + k) % 4) for s in range(4) for t in range(4)]


def write_coded(part_ref, code_ref, own_ref):
    rows, cols = own_ref.shape
    own_ref[...] = part_ref[:rows, :]
    diagonal = lax.broadcasted_iota(jnp.int32, (rows, rows), 0) == lax.broadcasted_iota(
        jnp.int32, (rows, rows), 1
    )
    for b in range(1, 4):
        part = part_ref[b * rows : (b + 1) * rows, :]
        top = jnp.max(jnp.abs(part), axis=1, keepdims=True)
        power = jnp.ceil(jnp.log(jnp.maximum(top, 1e-30)) * 1.4426950408889634 + 0.001)
        power = jnp.clip(power, -90.0, 126.0)
        code = jnp.floor(part * (jnp.exp(power * -0.6931471805599453) * TOP) + 0.5)
        code = jnp.clip(code, -32767.0, 32767.0)
        code_ref[b - 1, :rows, :] = code.astype(jnp.int32).astype(i16)
        across = jnp.sum(jnp.where(diagonal, power, 0.0), axis=0, keepdims=True)
        across = jnp.broadcast_to(across, (TAIL, rows))
        code_ref[b - 1, rows:, :rows] = across.astype(jnp.int32).astype(i16)
        if cols > rows:
            code_ref[b - 1, rows:, rows:] = jnp.zeros((TAIL, cols - rows), i16)


def in_hbm(n):
    return [pl.BlockSpec(memory_space=pltpu.HBM)] * n


def in_vmem(n):
    return [pl.BlockSpec(memory_space=pltpu.VMEM)] * n


def stay(a):
    return pltpu.with_memory_space_constraint(a, pltpu.HBM)


def keep(a):
    return pltpu.with_memory_space_constraint(a, pltpu.VMEM)


def fetch(pairs, sems):
    copies = [pltpu.make_async_copy(a, b, sems.at[i]) for i, (a, b) in enumerate(pairs)]
    for copy in copies:
        copy.start()
    return copies


def add_products(acc, source, head, copies):
    tile = head.shape[0] // len(copies)
    for i, copy in enumerate(copies):
        copy.wait()
        if i % 2:
            span = slice((i - 1) * tile, (i + 1) * tile)
            part = jnp.dot(source[:, span], head[span, :], preferred_element_type=f32)
            acc[...] = part if i == 1 else acc[...] + part


def teacher_kernel(
    ahead_ref, places_ref, mine_ref, other_ref, head_ref, code_ref, own_ref,
    mine, other, head, chosen, acc, mine_sems, other_sems, head_sems,
):
    half, width = mine_ref.shape
    parts = head_sems.shape[0]
    tile = width // parts
    spans = [pl.ds(i * tile, tile) for i in range(parts)]
    got_mine = fetch([(mine_ref.at[:, span], mine.at[:, span]) for span in spans], mine_sems)
    got_other = fetch([(other_ref.at[:, span], other.at[:, span]) for span in spans], other_sems)
    pick = (ahead_ref[...] == places_ref[...]).astype(f32).astype(bf16)
    for i, span in enumerate(spans):
        got_mine[i].wait()
        got_other[i].wait()
        if i == 0:
            copies = fetch([(head_ref.at[span], head.at[span]) for span in spans], head_sems)
        rows = jnp.dot(pick[:, :half], mine[:, span], preferred_element_type=f32)
        rows += jnp.dot(pick[:, half:], other[:, span], preferred_element_type=f32)
        chosen[:, span] = rows.astype(bf16)
    add_products(acc, chosen, head, copies)
    write_coded(acc, code_ref, own_ref)


def coded_shapes(rows, cols):
    return [
        jax.ShapeDtypeStruct((3, rows + TAIL, cols), i16),
        jax.ShapeDtypeStruct((rows, cols), f32),
    ]


def teacher_part(ahead, places, mine, other, head):
    tokens, (half, width), cols = ahead.shape[0], mine.shape, head.shape[1]
    parts = 4
    return pl.pallas_call(
        teacher_kernel,
        in_specs=in_vmem(2) + in_hbm(3),
        out_specs=in_vmem(2),
        out_shape=coded_shapes(tokens // 4, cols),
        scratch_shapes=[
            pltpu.VMEM((half, width), bf16),
            pltpu.VMEM((half, width), bf16),
            pltpu.VMEM((width, cols), bf16),
            pltpu.VMEM((tokens, width), bf16),
            pltpu.VMEM((tokens, cols), f32),
            pltpu.SemaphoreType.DMA((parts,)),
            pltpu.SemaphoreType.DMA((parts,)),
            pltpu.SemaphoreType.DMA((parts,)),
        ],
        compiler_params=pltpu.CompilerParams(vmem_limit_bytes=VMEM),
        cost_estimate=pl.CostEstimate(
            flops=2 * tokens * width * (cols + tokens),
            bytes_accessed=2 * width * (cols + tokens),
            transcendentals=0,
        ),
        name="teacher_part",
    )(ahead[:, None], places[None, :], stay(mine), stay(other), stay(head))


def student_kernel(
    order_ref, mine_ref, other_ref, head_ref, code_ref, own_ref, hidden, head, acc, head_sems
):
    blocks, _, feats = mine_ref.shape
    parts = head_sems.shape[0]
    tile = head.shape[0] // parts
    spans = [pl.ds(i * tile, tile) for i in range(parts)]
    copies = fetch([(head_ref.at[span], head.at[span]) for span in spans], head_sems)
    for i in range(2 * blocks):
        at = pl.multiple_of(order_ref[i] * feats, feats)
        source = mine_ref if i < blocks else other_ref
        hidden[:, pl.ds(at, feats)] = source[i % blocks]
    add_products(acc, hidden, head, copies)
    write_coded(acc, code_ref, own_ref)


def student_part(order, mine, other, head):
    (blocks, tokens, feats), (width, cols) = mine.shape, head.shape
    parts = 4
    return pl.pallas_call(
        student_kernel,
        in_specs=[pl.BlockSpec(memory_space=pltpu.SMEM)] + in_vmem(2) + in_hbm(1),
        out_specs=in_vmem(2),
        out_shape=coded_shapes(tokens // 4, cols),
        scratch_shapes=[
            pltpu.VMEM((tokens, width), bf16),
            pltpu.VMEM((width, cols), bf16),
            pltpu.VMEM((tokens, cols), f32),
            pltpu.SemaphoreType.DMA((parts,)),
        ],
        compiler_params=pltpu.CompilerParams(vmem_limit_bytes=VMEM),
        cost_estimate=pl.CostEstimate(
            flops=2 * tokens * width * cols,
            bytes_accessed=2 * width * (cols + tokens),
            transcendentals=0,
        ),
        name="student_part",
    )(order, mine, other, stay(head))


def bring_kernel(head_ref, out_ref, sems):
    for copy in fetch([(head_ref, out_ref)], sems):
        copy.wait()


def bring(head):
    return pl.pallas_call(
        bring_kernel,
        in_specs=in_hbm(1),
        out_specs=pl.BlockSpec(memory_space=pl.ANY),
        out_shape=jax.ShapeDtypeStruct(head.shape, head.dtype),
        scratch_shapes=[pltpu.SemaphoreType.DMA((1,))],
        compiler_params=pltpu.CompilerParams(vmem_limit_bytes=1024 * 1024),
        cost_estimate=pl.CostEstimate(
            flops=0, bytes_accessed=4 * head.shape[0] * head.shape[1], transcendentals=0
        ),
        name="bring",
    )(stay(head))


def gradient_kernel(
    where_ref, own_ref, front_ref, far0_ref, far1_ref, behind_ref, head_ref, out_ref,
    delta,
):
    rows, feats = out_ref.shape[3:]
    half = rows // 2
    core, x, y = where_ref[0], where_ref[1], where_ref[2]

    def put(ahead, start, source):
        at = pl.multiple_of(lax.rem(y + ahead, NY) * rows + start, half)
        delta[pl.ds(at, source.shape[0]), :] = source[...]

    put(0, 0, own_ref)
    put(1, 0, front_ref)
    put(2, 0, far0_ref)
    put(2, half, far1_ref)
    put(3, 0, behind_ref)
    for i in range(4):
        span = pl.ds(pl.multiple_of((2 * i + core) * 2 * feats, 2 * feats), 2 * feats)
        grad = lax.dot_general(
            delta[...], head_ref[span, :], (((1,), (1,)), ((), ())), preferred_element_type=f32
        ).astype(out_ref.dtype)
        for xl in range(2):
            ahead = lax.rem(2 * (i % 2) + xl + NX - x, NX)
            for a in range(4):
                out_ref[ahead, a, i // 2] = grad[
                    a * rows : (a + 1) * rows, xl * feats : (xl + 1) * feats
                ]


def gradient_part(core, x, y, pieces, head, dtype):
    (rows, cols), width = pieces[0].shape, head.shape[0]
    tokens, feats = 4 * rows, width // 16
    return pl.pallas_call(
        gradient_kernel,
        in_specs=[pl.BlockSpec(memory_space=pltpu.SMEM)] + in_vmem(len(pieces) + 1),
        out_specs=in_vmem(1)[0],
        scratch_shapes=[
            pltpu.VMEM((tokens, cols), bf16),
        ],
        out_shape=jax.ShapeDtypeStruct((4, 4, 2, rows, feats), dtype),
        compiler_params=pltpu.CompilerParams(vmem_limit_bytes=VMEM),
        cost_estimate=pl.CostEstimate(
            flops=tokens * width * cols,
            bytes_accessed=width * cols + 2 * tokens * cols,
            transcendentals=0,
        ),
        name="gradient_part",
    )(jnp.stack([core, x, y]).astype(jnp.int32), *pieces, keep(head))


def send_coded(code):
    return [shift(code[k - 1], "y", NY, k) for k in (2, 1, 3)]


def finish_sum(own, received):
    rows = own.shape[0]
    out = own
    for got in received:
        scale = jnp.exp2(got[rows, :rows].astype(f32)) * (1.0 / TOP)
        out = out + got[:rows].astype(f32) * scale[:, None]
    return out


def finish_kernel(got0_ref, got1_ref, got2_ref, own_ref, other_ref, rest_ref, exp_ref, sums_ref):
    rows = own_ref.shape[0]
    diagonal = lax.broadcasted_iota(jnp.int32, (rows, rows), 0) == lax.broadcasted_iota(
        jnp.int32, (rows, rows), 1
    )

    def upright(line):
        return jnp.sum(jnp.where(diagonal, line, 0.0), axis=1, keepdims=True)

    def lying(column):
        return jnp.sum(jnp.where(diagonal, column, 0.0), axis=0, keepdims=True)

    logit = own_ref[...]
    for got in (got0_ref, got1_ref, got2_ref):
        power = upright(got[rows:, :rows].astype(jnp.int32).astype(f32)[:1])
        scale = jnp.exp(power * 0.6931471805599453) * (1.0 / TOP)
        logit = logit + got[:rows, :].astype(jnp.int32).astype(f32) * scale
    exps = jnp.exp(logit - upright(rest_ref[...]))
    exp_ref[...] = exps
    sums_ref[:1, :] = lying(jnp.sum(exps, axis=1, keepdims=True))
    sums_ref[1:, :] = lying(jnp.sum(exps * (logit - other_ref[...]), axis=1, keepdims=True))


def finish_teacher(got, own, student_logit, rest):
    rows, cols = own.shape
    return pl.pallas_call(
        finish_kernel,
        in_specs=in_vmem(6),
        out_specs=in_vmem(2),
        out_shape=[jax.ShapeDtypeStruct((rows, cols), f32), jax.ShapeDtypeStruct((2, rows), f32)],
        compiler_params=pltpu.CompilerParams(vmem_limit_bytes=VMEM),
        cost_estimate=pl.CostEstimate(
            flops=20 * rows * cols, bytes_accessed=18 * rows * cols, transcendentals=rows * cols
        ),
        name="finish_teacher",
    )(*got, own, student_logit, rest[None, :])


def per_device(
    teacher_hidden,
    teacher_head,
    student_hidden,
    student_head,
    teacher_rest,
    student_rest,
    sampled,
    assign,
):
    y, zh, zl = lax.axis_index("y"), lax.axis_index("zh"), lax.axis_index("zl")
    x, c = lax.axis_index(X), lax.axis_index("c")
    tok_rows, feats = student_hidden.shape
    vocab_cols = student_head.shape[1]
    ahead = lax.dynamic_slice_in_dim(
        jnp.concatenate([assign, assign]), y * tok_rows, 4 * tok_rows, 0
    )
    xs = (x - jnp.arange(NX)) % NX

    n = teacher_hidden.shape[0]
    rows = [teacher_hidden] + [shift(teacher_hidden, X, NX, k) for k in range(1, NX)]
    mate = lax.ppermute(student_hidden, "zl", [(0, 1), (1, 0)])
    rows = jnp.concatenate(rows, 0)
    rows, student_hidden, mate = lax.optimization_barrier((rows, student_hidden, mate))
    rows = lax.all_gather(rows, Z, axis=0, tiled=True)

    got = jnp.stack([student_hidden, mate])
    got = jnp.stack([lax.ppermute(got, ("y", "zh"), swap_pairs(k)) for k in range(4)][::-1])
    got = turn(got, 3 - (zh - y) % 4, 4).transpose(1, 0, 2, 3).reshape(2, 4 * tok_rows, feats)
    got = [got] + [shift(got, X, NX, k) for k in (2, 1, 3)]
    got_other = jnp.concatenate([other_core(g) for g in got], 0)
    got = jnp.concatenate(got, 0)
    xo = (x - jnp.array([0, 2, 1, 3])) % NX
    quarter = jnp.stack([zl, 1 - zl])[None, :] * 8 + (xo // 2 * 4 + xo % 2)[:, None]
    order = (quarter[None] + jnp.stack([c, 1 - c])[:, None, None] * 2).reshape(-1)
    student_code, student_own = student_part(order, got, got_other, student_head)

    rows, student_code = lax.optimization_barrier((rows, student_code))
    student_got = send_coded(student_code)
    rows_other = other_core(rows)
    z_places = jnp.arange(NZ)[:, None] * 8 + (xs // 2 * 4 + xs % 2)[None, :]
    places = jnp.stack([z_places + 2 * c, z_places + 2 * (1 - c)])[..., None] * n + jnp.arange(n)
    teacher_code, teacher_own = teacher_part(
        ahead, places.reshape(-1), rows, rows_other, teacher_head
    )
    teacher_got = send_coded(teacher_code)
    student_got, teacher_got[0] = lax.optimization_barrier((student_got, teacher_got[0]))
    student_logit = finish_sum(student_own, student_got)

    position = lax.broadcasted_iota(jnp.int32, (1, sampled.shape[0]), 1)
    token_ids = jnp.sum(
        jnp.where(ahead[:tok_rows, None] == position, sampled[None, :], 0), axis=1
    )
    col_index = lax.axis_index(VOCAB) * vocab_cols + lax.broadcasted_iota(
        jnp.int32, (1, vocab_cols), 1
    )
    student_exp = jnp.exp(student_logit - student_rest[:, None])
    student_sums = jnp.stack(
        [
            jnp.sum(student_exp, axis=1),
            jnp.sum(jnp.where(col_index == token_ids[:, None], student_logit, 0.0), axis=1),
        ]
    )
    teacher_exp, teacher_sums = finish_teacher(
        teacher_got, teacher_own, student_logit, teacher_rest
    )
    sums = jnp.concatenate([teacher_sums, student_sums], 0)
    sums = lax.all_to_all(jnp.broadcast_to(sums[None], (64,) + sums.shape), VOCAB, 0, 0)
    teacher_total, gap, student_total, picked = jnp.sum(sums, axis=0)
    teacher_norm = teacher_rest + jnp.log(1.0 + teacher_total)
    student_norm = student_rest + jnp.log(1.0 + student_total)
    teacher_scale = 1.0 / (1.0 + teacher_total)
    student_scale = 1.0 / (1.0 + student_total)
    divergence = (gap - (teacher_norm - student_norm) * teacher_total) * teacher_scale
    sampled_logprob = picked - student_norm

    delta = (
        loss_scale * (student_exp * student_scale[:, None] - teacher_exp * teacher_scale[:, None])
    ).astype(bf16)
    half = tok_rows // 2
    delta, student_head = lax.optimization_barrier((delta, student_head))
    student_head = bring(student_head)
    far = shift(delta, "y", NY, 2)
    behind = shift(delta, "y", NY, 1)
    front = shift(delta, "y", NY, -1)
    pieces = [delta, front, far[:half], far[half:], behind]

    theirs = other_core(gradient_part(1 - c, x, y, pieces, student_head, bf16))
    mine = gradient_part(c, x, y, pieces, student_head, f32)
    both = mine + theirs.astype(f32)
    grad = both[0]
    for k in (2, 1, 3):
        grad = grad + shift(both[k].astype(bf16), X, NX, k).astype(f32)
    grad = lax.all_to_all(grad.astype(bf16).reshape(NZ, tok_rows, feats), Z, 0, 0)
    grad = jnp.sum(grad.astype(f32), axis=0).astype(bf16)
    hidden_grad = lax.ppermute(grad, ("y", "zh"), swap_pairs(0))
    return (hidden_grad, divergence, sampled_logprob)


def solution(mesh):
    fine = Mesh(np.asarray(mesh.devices).reshape(SIZES), AXES)
    return jax.shard_map(
        per_device,
        mesh=fine,
        in_specs=(
            P(VOCAB, "y"),
            P("y", VOCAB),
            P("y", VOCAB),
            P("y", VOCAB),
            P("y"),
            P("y"),
            P(),
            P(),
        ),
        out_specs=(P("y", VOCAB), P("y"), P("y")),
        check_vma=False,
    )
```
